128 devices in a mesh: group: 8 (over y, core), seq: 16 (over z, x).
Axes of the slice: x: 4, y: 4, z: 4, core: 2. Of those that a mesh axis runs over, the one named last changes fastest.
Arguments:
- query: bfloat16 [16384, 12288], P(('group', 'seq')), may hold values from -210 to 210, as said below
- latent_raw: bfloat16 [16384, 512], P(('group', 'seq')), may hold values from -6 to 6
- rope_raw: bfloat16 [16384, 64], P(('group', 'seq')), may hold values from -6 to 6
- kv_gain: float32 [512], replicated, may hold values from 0.1 to 1.9
- w_uk: bfloat16 [512, 8192], replicated, may hold values from -0.25 to 0.25
- w_uv: bfloat16 [512, 8192], replicated, may hold values from -0.25 to 0.25
- request_lengths: int32 [8, 32], P('group'), may hold values from 1 to 128, 2048 in all within a row
- page_owner: int32 [256], replicated, may hold values from 0 to 127, as said below
- page_slot: int32 [256], replicated, may hold values from 0 to 3, as said below
Outputs:
- attended: bfloat16 [16384, 8192], P(('group', 'seq'))
- decode_cache: bfloat16 [512, 36864], P(('group', 'seq'))
The draws below stay inside these ranges and needn't reach their ends.
Inputs may be any that keep to these rules, and one draw needn't show every extreme that they name: `request_lengths`: each row sums to 2048; no request is longer than 128 tokens. `query`: large rows may occur. `page_owner`: no owner gets more than 4 pages, and some owner gets exactly 4. `page_slot`: pages of one owner have distinct slots.
All inputs are finite; a program needn't handle non-finite values.
Results may differ from the reference program's by a relative error of at most 0.012.
The reference program's roundings to bfloat16 on the way (of `latent`, `key_rope`, `query_nope`, `query_rope` and `probs`) count: a program that leaves them out, or rounds other values in their place, can miss the bound.
Values may be sent and summed in bfloat16 or wider, within the bound.
A program may use at most 192 MiB of HBM per device.

```python
import math
import jax
import jax.numpy as jnp
import numpy as np
from jax import lax

HEADS = 64
NOPE = 128
ROPE = 64
VDIM = 128
LATENT = 512
T_DEV = 128
SEQ_LEN = 2048
GROUPS = 8
TOKENS = 16384
REQS = 32
OWNERS = 128
PAGES = 256
RECV_CAP = 4
PAGE_W = 36864


def pick_slots(key):
    total = OWNERS * RECV_CAP
    order = jax.random.permutation(key, total).astype(jnp.int32)
    filled = order[0] // RECV_CAP
    rank = jnp.zeros((total,), jnp.int32).at[order].set(jnp.arange(total, dtype=jnp.int32))
    owner_of = jnp.arange(total, dtype=jnp.int32) // RECV_CAP
    priority = jnp.where(owner_of == filled, 0, total) + rank
    chosen = jnp.argsort(priority, stable=True)[:PAGES].astype(jnp.int32)
    shuffle = jax.random.permutation(jax.random.fold_in(key, 11), PAGES)
    return chosen[shuffle].astype(jnp.int32)


def draw_page_owner(key, part):
    chosen = pick_slots(key)
    return (chosen // RECV_CAP).astype(jnp.int32)


def draw_page_slot(key, part):
    chosen = pick_slots(key)
    return (chosen % RECV_CAP).astype(jnp.int32)


def draw_query(key, part):
    key = jax.random.fold_in(key, 7)
    first = jax.random.fold_in(key, 0)
    shape = (TOKENS, HEADS * (NOPE + ROPE))
    values = jnp.clip(jax.random.normal(first, shape, jnp.float32), -6.0, 6.0)
    return values.astype(jnp.bfloat16)


def shard_levels(stream_key, shape, cuts, low, top_value):
    factor_of = 1.0
    for axis_at, blocks in cuts:
        draws = jax.random.uniform(jax.random.fold_in(jax.random.fold_in(stream_key, 6), axis_at), (blocks,), jnp.float32, low / len(cuts), top_value / len(cuts))
        factor_of = factor_of * jnp.repeat(jnp.exp(draws), shape[axis_at] // blocks).reshape((-1,) + (1,) * (len(shape) - 1 - axis_at))
    return factor_of


def profile(count, total, bound, lean):
    loads = [(1 << 20) // math.isqrt(grade ** lean) + 1 for grade in range(2, count + 1)]
    surplus, counts = total - bound - (count - 1), [1] * (count - 1)
    while surplus > 0:
        free = [i for i in range(count - 1) if counts[i] < bound]
        whole, remaining = sum([loads[i] for i in free]), surplus
        for i in free:
            addition = min(bound - counts[i], max(1, remaining * loads[i] // whole), surplus)
            counts[i] = counts[i] + addition
            surplus = surplus - addition
    return np.array([bound] + counts)


def ragged(rng, count, total, most, lean):
    if count == 2:
        one = jax.random.randint(rng, (), max(1, total - most), min(most, total - 1) + 1)
        return jnp.stack([one, total - one])
    tallies = jnp.asarray(profile(count, total, most, lean), jnp.int32)
    pairs = (count - 1) // 2
    giver, receiver = tallies[1:1 + 2 * pairs:2], tallies[2:2 + 2 * pairs:2]
    room = jnp.minimum(giver - 1, most - receiver)
    moved = jax.random.randint(jax.random.fold_in(rng, 1), (pairs,), 0, 1 << 20) % (room + 1)
    tallies = tallies.at[1:1 + 2 * pairs:2].set(giver - moved).at[2:2 + 2 * pairs:2].set(receiver + moved)
    return tallies[jax.random.permutation(jax.random.fold_in(rng, 2), count)]


def normal_values(rng, shape, width, bound, shards=(), held_as=jnp.bfloat16):
    result = jax.random.normal(rng, shape, jnp.float32) * width
    if len(shards) > 0:
        result = shard_levels(rng, shape, shards, -0.22, 0.18) * result
    return jnp.clip(result, min=-bound, max=bound).astype(held_as)


def setup_inputs(seed: int = 0) -> dict:
    key_of = jax.random.split(jax.random.key(seed), 10)
    return {
        "query": draw_query(jax.random.fold_in(key_of[9], 71), 0),
        "latent_raw": normal_values(key_of[1], (TOKENS, LATENT), 1.0, 6.0, ((0, 128),)),
        "rope_raw": normal_values(key_of[2], (TOKENS, ROPE), 1.0, 6.0, ((0, 128),)),
        "kv_gain": jnp.clip(1.0 + 0.18 * jax.random.normal(key_of[3], (LATENT,), jnp.float32), 0.1, 1.9),
        "w_uk": normal_values(key_of[4], (LATENT, HEADS * NOPE), LATENT ** -0.5, 0.25),
        "w_uv": normal_values(key_of[5], (LATENT, HEADS * VDIM), LATENT ** -0.5, 0.25),
        "request_lengths": jax.vmap(lambda own: ragged(own, REQS, SEQ_LEN, T_DEV, 2))(jax.random.split(key_of[6], GROUPS)).reshape((GROUPS, REQS)).astype(jnp.int32),
        "page_owner": draw_page_owner(jax.random.fold_in(key_of[9], 71), 0),
        "page_slot": draw_page_slot(jax.random.fold_in(key_of[9], 71), 0),
    }


def request_info(lengths, index):
    starts = jnp.cumsum(lengths) - lengths
    inside = starts[None, :] <= index[:, None]
    rid = lax.optimization_barrier(jnp.sum(inside.astype(jnp.int32), axis=1)).astype(jnp.int32) - 1
    begin = lax.optimization_barrier(jnp.max(jnp.where(inside, starts[None, :], 0), axis=1))
    return (rid, (index - begin).astype(jnp.int32))

def rotary(values, position):
    half = values.shape[-1] // 2
    freqs = 10000.0 ** (-jnp.arange(half, dtype=jnp.float32) / half)
    angle = position.astype(jnp.float32)[:, None] * freqs[None, :]
    shape = (values.shape[0],) + (1,) * (values.ndim - 2) + (half,)
    cosine = jnp.cos(angle).reshape(shape)
    sine = jnp.sin(angle).reshape(shape)
    first = values[..., :half]
    second = values[..., half:]
    return jnp.concatenate([first * cosine - second * sine, second * cosine + first * sine], -1)

def reference(query, latent_raw, rope_raw, kv_gain, w_uk, w_uv, request_lengths, page_owner, page_slot):
    index = jnp.arange(SEQ_LEN, dtype=jnp.int32)
    rid_all, pos_all = jax.vmap(lambda row: request_info(row, index))(request_lengths)
    groups = jnp.arange(GROUPS, dtype=jnp.int32)[:, None]
    rid = (rid_all + groups * REQS).reshape(TOKENS)
    pos = pos_all.reshape(TOKENS)
    source = latent_raw.astype(jnp.float32)
    scale_norm = lax.rsqrt(lax.optimization_barrier(jnp.mean(source * source, axis=1, keepdims=True)) + 1e-06)
    latent = (source * scale_norm * kv_gain[None, :]).astype(jnp.bfloat16)
    key_rope = rotary(rope_raw.astype(jnp.float32), pos).astype(jnp.bfloat16)
    key_nope = jnp.dot(latent, w_uk, preferred_element_type=jnp.float32).astype(jnp.bfloat16).reshape(TOKENS, HEADS, NOPE)
    value = jnp.dot(latent, w_uv, preferred_element_type=jnp.float32).astype(jnp.bfloat16).reshape(TOKENS, HEADS, VDIM)
    shaped = query.reshape(TOKENS, HEADS, NOPE + ROPE)
    query_nope = shaped[:, :, :NOPE]
    query_rope = rotary(shaped[:, :, NOPE:].astype(jnp.float32), pos).astype(jnp.bfloat16)
    factor = 1.0 / (NOPE + ROPE) ** 0.5

    def block(number):
        qstart = (number * T_DEV).astype(jnp.int32)
        kstart = (jnp.maximum(number - 1, 0) * T_DEV).astype(jnp.int32)
        qn = lax.dynamic_slice_in_dim(query_nope, qstart, T_DEV, 0).astype(jnp.float32)
        qr = lax.dynamic_slice_in_dim(query_rope, qstart, T_DEV, 0).astype(jnp.float32)
        kn = lax.dynamic_slice_in_dim(key_nope, kstart, 2 * T_DEV, 0).astype(jnp.float32)
        kr = lax.dynamic_slice_in_dim(key_rope, kstart, 2 * T_DEV, 0).astype(jnp.float32)
        vv = lax.dynamic_slice_in_dim(value, kstart, 2 * T_DEV, 0).astype(jnp.float32)
        rq = lax.dynamic_slice_in_dim(rid, qstart, T_DEV, 0)
        rk = lax.dynamic_slice_in_dim(rid, kstart, 2 * T_DEV, 0)
        tq = qstart + jnp.arange(T_DEV, dtype=jnp.int32)
        tk = kstart + jnp.arange(2 * T_DEV, dtype=jnp.int32)
        allowed = (rq[:, None] == rk[None, :]) & (tk[None, :] <= tq[:, None])
        score = (jnp.einsum('thd,uhd->thu', qn, kn) + jnp.einsum('thd,ud->thu', qr, kr)) * factor
        score = jnp.where(allowed[:, None, :], score, -1e+30)
        top = lax.optimization_barrier(jnp.max(score, axis=2, keepdims=True))
        weights = jnp.where(allowed[:, None, :], jnp.exp(score - top), 0.0)
        probs = (weights / lax.optimization_barrier(jnp.sum(weights, axis=2, keepdims=True))).astype(jnp.bfloat16)
        out = jnp.einsum('thu,uhd->thd', probs.astype(jnp.float32), vv)
        return out.astype(jnp.bfloat16).reshape(T_DEV, HEADS * VDIM)
    blocks = lax.map(block, jnp.arange(TOKENS // T_DEV, dtype=jnp.int32))
    attended = blocks.reshape(TOKENS, HEADS * VDIM)
    pages = jnp.concatenate([latent, key_rope], axis=1).reshape(PAGES, PAGE_W)
    target = (page_owner * RECV_CAP + page_slot).astype(jnp.int32)
    cache = jnp.zeros((OWNERS * RECV_CAP, PAGE_W), jnp.bfloat16).at[target].set(pages)
    return (attended, cache)
```

```python
import functools

import jax
import jax.numpy as jnp
import numpy as np
from jax import lax
from jax.experimental import pallas as pl
from jax.experimental.pallas import tpu as pltpu
from jax.sharding import PartitionSpec as P
import ml_dtypes

MESH = pl.DeviceIdType.MESH
F32 = jnp.float32
BF16 = jnp.bfloat16
TOK = 128
HEADS = 64
LATENT = 512
QUADS = 16
TILES = 5
CHUNKS = QUADS * TILES
STEPS = 16
FIRST = 11
PAGE_W = 36864
SCALE = float(1.0 / 192.0**0.5 * np.log2(np.e))


def trig_table():
    freqs = (10000.0 ** (-np.arange(32, dtype=np.float64) / 32.0)).astype(np.float32)
    angle = np.arange(TOK, dtype=np.float32)[:, None] * freqs[None, :]
    cosine = np.cos(angle.astype(np.float64)).astype(np.float32)
    sine = np.sin(angle.astype(np.float64)).astype(np.float32)
    full = np.concatenate([cosine] * 4 + [-sine, sine, -sine, sine], axis=1)
    parts = []
    for _ in range(3):
        part = full.astype(ml_dtypes.bfloat16)
        parts.append(part)
        full = full - part.astype(np.float32)
    return np.concatenate(parts, axis=0)


def middle_of(quad, tile):
    if tile < 4:
        return (2 * tile, quad)
    return (2 * ((8 - quad // 4 - quad % 4) % 4) + 1, quad)


def remote(src, dst, send, recv, device):
    return pltpu.make_async_remote_copy(
        src_ref=src, dst_ref=dst, send_sem=send, recv_sem=recv, device_id=device, device_id_type=MESH
    )


def done(ref, sem):
    pltpu.make_async_copy(ref, ref, sem).wait()


def rotated(x, cosine, sine, low):
    partner = jnp.where(low, pltpu.roll(x, 96, 1), pltpu.roll(x, 32, 1))
    return x * cosine + partner * sine


def kernel(
    lengths, latent_raw, rope_raw, gain, owner, slot, trig, query, w_uk, w_uv,
    out, cache,
    qv, kv, vv, ov, lat2, kr2, krh, cos_v, sin_v, bias, ypage, xs, rs, rf, of, os, cb, cf, cout, onehot,
    q_sem, k_sem, v_sem, o_sem, send_n, recv_n, send1, recv1, send2, recv2, c_sem,
):
    g, s = lax.axis_index("group"), lax.axis_index("seq")
    me = g * 16 + s
    core, y = g % 2, g // 2
    diagonal = (s // 4 + s % 4 + y) % 4 == 0
    middle = (core == 0) | diagonal
    my_tile = jnp.where(core == 0, y, 4)
    my_chunk = s * TILES + my_tile
    has_left, has_right = s > 0, s < 15

    barrier = pltpu.get_barrier_semaphore()

    def greet(device):
        pl.semaphore_signal(barrier, inc=1, device_id=device, device_id_type=MESH)

    @pl.when(middle)
    def _():
        for quad in range(QUADS):
            for row in range(4):
                if (quad // 4 + quad % 4 + row) % 4 != 0:
                    greet((2 * row + 1, quad))

    def each_middle(act):
        for step in range(QUADS):
            quad = (s + step) % 16
            for tile in range(TILES):
                device = middle_of(quad, tile)
                if step:
                    act(quad, tile, device)
                else:
                    pl.when(device[0] != g)(functools.partial(act, quad, tile, device))

    each_middle(lambda quad, tile, device: greet(device))

    @pl.when(has_left)
    def _():
        greet((g, s - 1))

    def fetches(i):
        return (
            pltpu.make_async_copy(query.at[:, pl.ds(i * 768, 768)], qv.at[i], q_sem.at[i]),
            pltpu.make_async_copy(w_uk.at[:, pl.ds(i * 512, 512)], kv.at[i], k_sem.at[i]),
            pltpu.make_async_copy(w_uv.at[:, pl.ds(i * 512, 512)], vv.at[i], v_sem.at[i]),
        )

    for i in range(STEPS):
        for fetch in fetches(i):
            fetch.start()

    row = lax.broadcasted_iota(jnp.int32, (TOK, TOK), 0)
    col = lax.broadcasted_iota(jnp.int32, (TOK, TOK), 1)
    low = col % 64 < 32
    half = col < 64
    index = row + s * TOK
    begin = jnp.zeros((TOK, TOK), jnp.int32)
    start = jnp.int32(0)
    for r in range(32):
        begin = jnp.where(index >= start, start, begin)
        start = start + lengths[0, r]
    pos = index - begin
    hot = (col == pos).astype(F32).astype(BF16)
    angles = jnp.dot(jnp.concatenate([hot, hot, hot], axis=1), trig[...], preferred_element_type=F32)
    cosine, sine = angles[:, :TOK], angles[:, TOK:]
    cos_v[...] = cosine
    sin_v[...] = sine
    bias[...] = jnp.where((row - col + TOK) % TOK <= pos, 0.0, -1e30)

    source = latent_raw[...].astype(F32)
    norm = lax.rsqrt(jnp.mean(source * source, axis=1, keepdims=True) + 1e-06)
    latent = (source * norm * gain[...]).astype(BF16)
    lat2[TOK:, :] = latent
    rope = rope_raw[...].astype(F32)
    key_rope = rotated(jnp.concatenate([rope, rope], axis=1), cosine, sine, low).astype(BF16)
    kr2[TOK:, :] = key_rope

    wide, tail = latent.astype(F32), key_rope.astype(F32)
    plain = [wide[:, i * 128 : (i + 1) * 128] for i in range(4)]
    turned = [pltpu.roll(x, 64, 1) for x in plain]
    moved = (
        [turned[0]]
        + [jnp.where(half, turned[i - 1], turned[i]) for i in range(1, 4)]
        + [jnp.where(half, turned[3], tail)]
    )
    odd = row % 2 == 1
    upper = lax.broadcasted_iota(jnp.int32, (8, 128), 0) < 4
    for tile, (a, b) in enumerate(zip(plain + [tail], moved)):
        ypage[tile] = jnp.where(odd, b, a)
    for tile in range(TILES):
        for octet in range(8):
            first = ypage[tile, octet * 8 : octet * 8 + 8, :]
            second = ypage[tile, 64 + octet * 8 : 64 + octet * 8 + 8, :]
            xs[2 * octet * TILES + tile] = jnp.where(upper, first, pltpu.roll(second, 4, 0)).astype(BF16)
            xs[(2 * octet + 1) * TILES + tile] = jnp.where(upper, pltpu.roll(first, 4, 0), second).astype(BF16)

    pl.semaphore_wait(barrier, jnp.where(middle, 127, CHUNKS) + jnp.where(has_right, 1, 0))

    lat_copy = remote(lat2.at[pl.ds(TOK, TOK)], lat2.at[pl.ds(0, TOK)], send_n.at[0], recv_n.at[0], (g, s + 1))
    rope_copy = remote(kr2.at[pl.ds(TOK, TOK)], kr2.at[pl.ds(0, TOK)], send_n.at[1], recv_n.at[1], (g, s + 1))

    @pl.when(has_right)
    def _():
        lat_copy.start()
        rope_copy.start()

    each_middle(
        lambda quad, tile, device: remote(xs.at[quad * TILES + tile], rs.at[me], send1, recv1, device).start()
    )

    @pl.when(middle)
    def _():
        rs[me] = xs[my_chunk]
        want = slot[...] * 128 + owner[...]
        onehot[...] = (lax.broadcasted_iota(jnp.int32, (512, 256), 0) == want).astype(F32).astype(BF16)

    @pl.when(has_left)
    def _():
        done(lat2.at[pl.ds(0, TOK)], recv_n.at[0])
        done(kr2.at[pl.ds(0, TOK)], recv_n.at[1])

    @pl.when(s == 0)
    def _():
        lat2[:TOK, :] = jnp.zeros((TOK, LATENT), BF16)
        kr2[:TOK, :] = jnp.zeros((TOK, TOK), BF16)

    half2 = lax.broadcasted_iota(jnp.int32, (2 * TOK, TOK), 1) < 64
    ropes = kr2[...].astype(F32)
    krh[0] = jnp.where(half2, ropes, 0.0).astype(BF16)
    krh[1] = jnp.where(half2, 0.0, ropes).astype(BF16)

    def attend(i):
        for fetch in fetches(i):
            fetch.wait()
        keys = jnp.dot(lat2[...], kv[i], preferred_element_type=F32).astype(BF16)
        values = jnp.dot(lat2[...], vv[i], preferred_element_type=F32).astype(BF16)
        row = lax.broadcasted_iota(jnp.int32, (TOK, TOK), 0)
        col = lax.broadcasted_iota(jnp.int32, (TOK, TOK), 1)
        own = col <= row
        half = col < 64
        low = col % 64 < 32
        for pair in range(2):
            tiles = [qv[i, :, pl.ds(pair * 384 + t * 128, 128)].astype(F32) for t in range(3)]
            turn = rotated(jnp.where(half, tiles[1], tiles[2]), cos_v[...], sin_v[...], low).astype(BF16)
            second = pltpu.roll(jnp.where(half, tiles[2], tiles[1]), 64, 1).astype(BF16)
            for one, nope in enumerate((tiles[0].astype(BF16), second)):
                h = 2 * pair + one
                left = jnp.concatenate([nope, turn], axis=1)
                right = jnp.concatenate([keys[:, h * 128 : (h + 1) * 128], krh[one]], axis=1)
                score = lax.dot_general(left, right, (((1,), (1,)), ((), ())), preferred_element_type=F32)
                score = jnp.where(own, score[:, TOK:], score[:, :TOK]) + bias[...]
                top = jnp.max(score, axis=1, keepdims=True)
                weight = jnp.exp2((score - top) * SCALE)
                probs = weight * (1.0 / jnp.sum(weight, axis=1, keepdims=True))
                both = jnp.concatenate(
                    [jnp.where(own, 0.0, probs).astype(BF16), jnp.where(own, probs, 0.0).astype(BF16)], axis=1
                )
                got = jnp.dot(both, values[:, h * 128 : (h + 1) * 128], preferred_element_type=F32)
                ov[i, :, h * 128 : (h + 1) * 128] = got.astype(BF16)
        pltpu.make_async_copy(ov.at[i], out.at[:, pl.ds(i * 512, 512)], o_sem.at[i]).start()

    @pl.loop(0, FIRST)
    def _(i):
        attend(i)

    @pl.when(middle)
    def _():
        done(rs.at[pl.ds(0, 127)], recv1)
        rf[...] = rs[...].astype(F32).reshape(1024, 128)
        pages = jnp.concatenate([rf[pl.ds(t, 256, stride=4), :].astype(BF16) for t in range(4)], axis=1)
        picked = jnp.dot(onehot[...], pages, preferred_element_type=F32)
        for t in range(4):
            for k in range(4):
                of[pl.ds(t * 4 + k, 128, stride=16), :] = picked[k * 128 : (k + 1) * 128, t * 128 : (t + 1) * 128]
        os[...] = of[...].reshape(128, 16, 128).astype(BF16)
        for dg in range(8):
            for ds in range(16):
                if dg + ds:
                    a, b = (g + dg) % 8, (s + ds) % 16
                    remote(os.at[a * 16 + b], cb.at[my_chunk], send2, recv2, (a, b)).start()
        cb[my_chunk] = os[me]

    @pl.loop(FIRST, STEPS)
    def _(i):
        attend(i)

    @pl.when(middle)
    def _():
        done(cb.at[pl.ds(0, CHUNKS - 1)], recv2)

    @pl.when(jnp.logical_not(middle))
    def _():
        done(cb, recv2)

    cf[...] = cb[...].astype(F32).reshape(CHUNKS * 16, 128)
    half4 = lax.broadcasted_iota(jnp.int32, (4, 128), 1) < 64
    for quad in range(QUADS):
        for two in range(2):
            base = (quad * 2 + two) * 9

            def piece(tile, odd):
                return cf[pl.ds((quad * TILES + tile) * 16 + (2 * two + odd) * 4, 4), :]

            parts = (
                [piece(tile, 0) for tile in range(4)]
                + [jnp.where(half4, piece(4, 0), piece(0, 1))]
                + [piece(tile, 1) for tile in range(1, 5)]
            )
            for k, part in enumerate(parts):
                cout[:, (base + k) * 128 : (base + k + 1) * 128] = part.astype(BF16)
    last = pltpu.make_async_copy(cout, cache, c_sem)
    last.start()

    @pl.when(middle)
    def _():
        done(xs.at[pl.ds(0, CHUNKS - 1)], send1)
        done(os.at[pl.ds(0, 127)], send2)

    @pl.when(jnp.logical_not(middle))
    def _():
        done(xs, send1)

    @pl.when(has_right)
    def _():
        lat_copy.wait_send()
        rope_copy.wait_send()

    for i in range(STEPS):
        pltpu.make_async_copy(ov.at[i], out.at[:, pl.ds(i * 512, 512)], o_sem.at[i]).wait()
    last.wait()


def on_device(query, latent_raw, rope_raw, kv_gain, w_uk, w_uv, request_lengths, page_owner, page_slot):
    vmem = pl.BlockSpec(memory_space=pltpu.VMEM)
    anywhere = pl.BlockSpec(memory_space=pl.ANY)
    dma = pltpu.SemaphoreType.DMA
    return pl.pallas_call(
        kernel,
        out_shape=(
            jax.ShapeDtypeStruct((TOK, HEADS * 128), BF16),
            jax.ShapeDtypeStruct((4, PAGE_W), BF16),
        ),
        in_specs=[pl.BlockSpec(memory_space=pltpu.SMEM)] + [vmem] * 6 + [anywhere] * 3,
        out_specs=(anywhere, anywhere),
        scratch_shapes=[
            pltpu.VMEM((STEPS, TOK, 768), BF16),
            pltpu.VMEM((STEPS, LATENT, 512), BF16),
            pltpu.VMEM((STEPS, LATENT, 512), BF16),
            pltpu.VMEM((STEPS, TOK, 512), BF16),
            pltpu.VMEM((2 * TOK, LATENT), BF16),
            pltpu.VMEM((2 * TOK, TOK), BF16),
            pltpu.VMEM((2, 2 * TOK, TOK), BF16),
            pltpu.VMEM((TOK, TOK), F32),
            pltpu.VMEM((TOK, TOK), F32),
            pltpu.VMEM((TOK, TOK), F32),
            pltpu.VMEM((TILES, TOK, 128), F32),
            pltpu.VMEM((CHUNKS, 8, 128), BF16),
            pltpu.VMEM((128, 8, 128), BF16),
            pltpu.VMEM((1024, 128), F32),
            pltpu.VMEM((2048, 128), F32),
            pltpu.VMEM((128, 16, 128), BF16),
            pltpu.VMEM((CHUNKS, 16, 128), BF16),
            pltpu.VMEM((CHUNKS * 16, 128), F32),
            pltpu.VMEM((4, PAGE_W), BF16),
            pltpu.VMEM((512, 256), BF16),
            dma((STEPS,)),
            dma((STEPS,)),
            dma((STEPS,)),
            dma((STEPS,)),
            dma((2,)),
            dma((2,)),
            dma,
            dma,
            dma,
            dma,
            dma,
        ],
        compiler_params=pltpu.CompilerParams(
            collective_id=0, has_side_effects=True, vmem_limit_bytes=48 * 2**20
        ),
        name="prefill_and_pages",
    )(
        request_lengths,
        latent_raw,
        rope_raw,
        kv_gain.reshape(1, LATENT),
        page_owner.reshape(1, 256),
        page_slot.reshape(1, 256),
        jnp.asarray(trig_table()),
        query,
        w_uk,
        w_uv,
    )


def solution(mesh):
    rows = P(("group", "seq"), None)
    return jax.shard_map(
        on_device,
        mesh=mesh,
        in_specs=(rows, rows, rows, P(), P(), P(), P("group", None), P(), P()),
        out_specs=(rows, rows),
        check_vma=False,
    )
```

```python
import functools

import jax
import jax.numpy as jnp
import numpy as np
from jax import lax
from jax.experimental import pallas as pl
from jax.experimental.pallas import tpu as pltpu
from jax.sharding import PartitionSpec as P
import ml_dtypes

MESH = pl.DeviceIdType.MESH
F32 = jnp.float32
BF16 = jnp.bfloat16
TOK = 128
HEADS = 64
LATENT = 512
QUADS = 16
TILES = 5
CHUNKS = QUADS * TILES
STEPS = 8
WIDE = 1024
QWIDE = 1536
HEADS_STEP = 8
SPLIT = 2
PAGE_W = 36864
SCALE = float(1.0 / 192.0**0.5 * np.log2(np.e))


def trig_table():
    freqs = (10000.0 ** (-np.arange(32, dtype=np.float64) / 32.0)).astype(np.float32)
    angle = np.arange(TOK, dtype=np.float32)[:, None] * freqs[None, :]
    cosine = np.cos(angle.astype(np.float64)).astype(np.float32)
    sine = np.sin(angle.astype(np.float64)).astype(np.float32)
    full = np.concatenate([cosine] * 4 + [-sine, sine, -sine, sine], axis=1)
    parts = []
    for _ in range(3):
        part = full.astype(ml_dtypes.bfloat16)
        parts.append(part)
        full = full - part.astype(np.float32)
    return np.concatenate(parts, axis=0)


def middle_of(quad, tile):
    if tile < 4:
        return (2 * tile, quad)
    return (2 * ((8 - quad // 4 - quad % 4) % 4) + 1, quad)


def remote(src, dst, send, recv, device):
    return pltpu.make_async_remote_copy(
        src_ref=src, dst_ref=dst, send_sem=send, recv_sem=recv, device_id=device, device_id_type=MESH
    )


def done(ref, sem):
    pltpu.make_async_copy(ref, ref, sem).wait()


def rotated(x, cosine, sine, low):
    partner = jnp.where(low, pltpu.roll(x, 96, 1), pltpu.roll(x, 32, 1))
    return x * cosine + partner * sine


def kernel(
    lengths, gain, latent_raw, rope_raw, trig, owner, slot, query, w_uk, w_uv,
    out, cache,
    lengths_s, gain_v, latent_v, rope_v, trig_v, owner_v, slot_v,
    qv, kv, vv, ov, lat2, kr2, cos_v, sin_v, bias, low_m, up_m, ypage, xs, rs, rf, of, os, cb, cf, cout, onehot,
    left0, left1, right0, right1, value0, value1, score_v, prob_v,
    in_sem, q_sem, k_sem, v_sem, o_sem, send_n, recv_n, send1, recv1, send2, recv2, c_sem,
):
    lefts, rights, valued = (left0, left1), (right0, right1), (value0, value1)
    g, s = lax.axis_index("group"), lax.axis_index("seq")
    me = g * 16 + s
    core, y = g % 2, g // 2
    diagonal = (s // 4 + s % 4 + y) % 4 == 0
    middle = (core == 0) | diagonal
    my_tile = jnp.where(core == 0, y, 4)
    my_chunk = s * TILES + my_tile
    has_left, has_right = s > 0, s < 15

    small = [
        pltpu.make_async_copy(src, dst, in_sem.at[i])
        for i, (src, dst) in enumerate(
            (
                (latent_raw, latent_v),
                (lengths, lengths_s),
                (rope_raw, rope_v),
                (trig, trig_v),
                (gain, gain_v),
                (owner, owner_v),
                (slot, slot_v),
            )
        )
    ]
    for copy in small:
        copy.start()

    def fetches(i):
        return (
            pltpu.make_async_copy(query.at[:, pl.ds(i * QWIDE, QWIDE)], qv.at[i], q_sem.at[i]),
            pltpu.make_async_copy(w_uk.at[:, pl.ds(i * WIDE, WIDE)], kv.at[i], k_sem.at[i]),
            pltpu.make_async_copy(w_uv.at[:, pl.ds(i * WIDE, WIDE)], vv.at[i], v_sem.at[i]),
        )

    def fetched(i):
        for fetch in fetches(i):
            fetch.wait()

    barrier = pltpu.get_barrier_semaphore()

    def greet(device):
        pl.semaphore_signal(barrier, inc=1, device_id=device, device_id_type=MESH)

    @pl.when(middle)
    def _():
        for quad in range(QUADS):
            for row in range(4):
                if (quad // 4 + quad % 4 + row) % 4 != 0:
                    greet((2 * row + 1, quad))

    def each_middle(act):
        for step in range(QUADS):
            quad = (s + step) % 16
            for tile in range(TILES):
                device = middle_of(quad, tile)
                if step:
                    act(quad, tile, device)
                else:
                    pl.when(device[0] != g)(functools.partial(act, quad, tile, device))

    each_middle(lambda quad, tile, device: greet(device))

    @pl.when(has_left)
    def _():
        greet((g, s - 1))

    for i in range(STEPS):
        for fetch in fetches(i):
            fetch.start()

    row = lax.broadcasted_iota(jnp.int32, (TOK, TOK), 0)
    col = lax.broadcasted_iota(jnp.int32, (TOK, TOK), 1)
    low = col % 64 < 32
    half = col < 64
    index = row + s * TOK
    for copy in small[:2]:
        copy.wait()
    begin = jnp.zeros((TOK, TOK), jnp.int32)
    start = jnp.int32(0)
    for r in range(32):
        begin = jnp.where(index >= start, start, begin)
        start = start + lengths_s[0, r]
    pos = index - begin
    hot = (col == pos).astype(F32).astype(BF16)
    for copy in small[2:]:
        copy.wait()
    angles = jnp.dot(jnp.concatenate([hot, hot, hot], axis=1), trig_v[...], preferred_element_type=F32)
    cosine, sine = angles[:, :TOK], angles[:, TOK:]
    cos_v[...] = cosine
    sin_v[...] = sine

    source = latent_v[...].astype(F32)
    norm = lax.rsqrt(jnp.mean(source * source, axis=1, keepdims=True) + 1e-06)
    latent = (source * norm * gain_v[...]).astype(BF16)
    lat2[TOK:, :] = latent
    rope = rope_v[...].astype(F32)
    rope = jnp.concatenate([rope, rope], axis=0).T
    key_rope = rotated(rope, cosine, sine, low).astype(BF16)
    kr2[TOK:, :] = key_rope

    wide, tail = latent.astype(F32), key_rope.astype(F32)
    plain = [wide[:, i * 128 : (i + 1) * 128] for i in range(4)]
    turned = [pltpu.roll(x, 64, 1) for x in plain]
    moved = (
        [turned[0]]
        + [jnp.where(half, turned[i - 1], turned[i]) for i in range(1, 4)]
        + [jnp.where(half, turned[3], tail)]
    )
    odd = row % 2 == 1
    upper = lax.broadcasted_iota(jnp.int32, (8, 128), 0) < 4
    for tile, (a, b) in enumerate(zip(plain + [tail], moved)):
        ypage[tile] = jnp.where(odd, b, a)
    for tile in range(TILES):
        for octet in range(8):
            first = ypage[tile, octet * 8 : octet * 8 + 8, :]
            second = ypage[tile, 64 + octet * 8 : 64 + octet * 8 + 8, :]
            xs[2 * octet * TILES + tile] = jnp.where(upper, first, pltpu.roll(second, 4, 0)).astype(BF16)
            xs[(2 * octet + 1) * TILES + tile] = jnp.where(upper, pltpu.roll(first, 4, 0), second).astype(BF16)

    pl.semaphore_wait(barrier, jnp.where(middle, 127, CHUNKS) + jnp.where(has_right, 1, 0))

    lat_copy = remote(lat2.at[pl.ds(TOK, TOK)], lat2.at[pl.ds(0, TOK)], send_n.at[0], recv_n.at[0], (g, s + 1))
    rope_copy = remote(kr2.at[pl.ds(TOK, TOK)], kr2.at[pl.ds(0, TOK)], send_n.at[1], recv_n.at[1], (g, s + 1))

    @pl.when(has_right)
    def _():
        lat_copy.start()
        rope_copy.start()

    each_middle(
        lambda quad, tile, device: remote(xs.at[quad * TILES + tile], rs.at[me], send1, recv1, device).start()
    )

    bias[...] = jnp.where((row - col + TOK) % TOK <= pos, 0.0, -1e30)
    low_m[...] = jnp.where(col <= row, 1.0, 0.0).astype(BF16)
    up_m[...] = jnp.where(col <= row, 0.0, 1.0).astype(BF16)
    for value in valued:
        value[:, :, TOK:] = jnp.ones((HEADS_STEP, 2 * TOK, TOK), BF16)

    @pl.when(middle)
    def _():
        rs[me] = xs[my_chunk]
        want = slot_v[...] * 128 + owner_v[...]
        onehot[...] = (lax.broadcasted_iota(jnp.int32, (512, 256), 0) == want).astype(F32).astype(BF16)

    @pl.when(has_left)
    def _():
        done(lat2.at[pl.ds(0, TOK)], recv_n.at[0])
        done(kr2.at[pl.ds(0, TOK)], recv_n.at[1])

    @pl.when(s == 0)
    def _():
        lat2[:TOK, :] = jnp.zeros((TOK, LATENT), BF16)
        kr2[:TOK, :] = jnp.zeros((TOK, TOK), BF16)

    ropes = kr2[...].astype(F32).T
    first_half = lax.broadcasted_iota(jnp.int32, (TOK, 2 * TOK), 0) < 64
    for one in range(2):
        masked = jnp.where(first_half if one == 0 else ~first_half, ropes, 0.0).astype(BF16)
        for right in rights:
            for pair in range(HEADS_STEP // 2):
                right[2 * pair + one, TOK:, :] = masked

    def prepare(i, b):
        col = lax.broadcasted_iota(jnp.int32, (TOK, TOK), 1)
        half = col < 64
        low = col % 64 < 32
        for pair in range(HEADS_STEP // 2):
            columns = slice(pair * 256, pair * 256 + 256)
            keys = jnp.dot(lat2[...], kv[i, :, columns], preferred_element_type=F32).astype(BF16)
            values = jnp.dot(lat2[...], vv[i, :, columns], preferred_element_type=F32).astype(BF16)
            for one in range(2):
                rights[b][2 * pair + one, :TOK, :] = keys[:, one * 128 : one * 128 + 128].T
                valued[b][2 * pair + one, :, :TOK] = values[:, one * 128 : one * 128 + 128]
            t0, t1, t2 = [qv[i, :, pl.ds(pair * 384 + t * 128, 128)] for t in range(3)]
            ropes = jnp.where(half, t1, t2).astype(F32)
            turn = rotated(ropes, cos_v[...], sin_v[...], low).astype(BF16)
            second = pltpu.roll(jnp.where(half, t2, t1).astype(F32), 64, 1).astype(BF16)
            for one, nope in enumerate((t0, second)):
                lefts[b][2 * pair + one, :, :TOK] = nope
                lefts[b][2 * pair + one, :, TOK:] = turn

    def scored(b, h):
        row = lax.broadcasted_iota(jnp.int32, (TOK, TOK), 0)
        col = lax.broadcasted_iota(jnp.int32, (TOK, TOK), 1)
        score = jnp.dot(lefts[b][h], rights[b][h], preferred_element_type=F32)
        score_v[h] = jnp.where(col <= row, score[:, TOK:], score[:, :TOK]) + bias[...]

    def softened(h):
        score = score_v[h]
        top = jnp.max(score, axis=1, keepdims=True)
        weight = jnp.exp2((score - top) * SCALE).astype(BF16)
        prob_v[h, :, :TOK] = weight * up_m[...]
        prob_v[h, :, TOK:] = weight * low_m[...]

    def summed(i, b, h):
        got = jnp.dot(prob_v[h], valued[b][h], preferred_element_type=F32)
        ov[i, :, h * 128 : (h + 1) * 128] = (got[:, :TOK] * (1.0 / got[:, TOK:])).astype(BF16)

    def result(i):
        return pltpu.make_async_copy(ov.at[i], out.at[:, pl.ds(i * WIDE, WIDE)], o_sem.at[i])

    def step(i, b):
        if b == 0:
            fetched(i + 1)
        else:
            pl.when(i + 1 < STEPS)(lambda: fetched(i + 1))
        for h in range(HEADS_STEP + 4):
            if h < HEADS_STEP:
                scored(b, h)
            if 0 <= h - 2 < HEADS_STEP:
                softened(h - 2)
            if 0 <= h - 4 < HEADS_STEP:
                summed(i, b, h - 4)
        prepare(jnp.minimum(i + 1, STEPS - 1), 1 - b)
        result(i).start()

    fetched(0)
    prepare(0, 0)

    @pl.loop(0, SPLIT)
    def _(j):
        for b in range(2):
            step(2 * j + b, b)

    @pl.when(middle)
    def _():
        done(rs.at[pl.ds(0, 127)], recv1)
        rf[...] = rs[...].astype(F32).reshape(1024, 128)
        pages = jnp.concatenate([rf[pl.ds(t, 256, stride=4), :].astype(BF16) for t in range(4)], axis=1)
        picked = jnp.dot(onehot[...], pages, preferred_element_type=F32)
        for t in range(4):
            for k in range(4):
                of[pl.ds(t * 4 + k, 128, stride=16), :] = picked[k * 128 : (k + 1) * 128, t * 128 : (t + 1) * 128]
        os[...] = of[...].reshape(128, 16, 128).astype(BF16)
        cb[my_chunk] = os[me]

    groups = 8 // (2 * (STEPS // 2 - SPLIT))

    @pl.loop(SPLIT, STEPS // 2)
    def _(j):
        for b in range(2):

            @pl.when(middle)
            def _():
                for k in range(groups):
                    dg = ((j - SPLIT) * 2 + b) * groups + k
                    for ds in range(16):
                        a, c = (g + dg) % 8, (s + ds) % 16
                        send = remote(os.at[a * 16 + c], cb.at[my_chunk], send2, recv2, (a, c))
                        if ds:
                            send.start()
                        else:
                            pl.when(dg > 0)(send.start)

            step(2 * j + b, b)

    @pl.when(middle)
    def _():
        done(cb.at[pl.ds(0, CHUNKS - 1)], recv2)

    @pl.when(jnp.logical_not(middle))
    def _():
        done(cb, recv2)

    cf[...] = cb[...].astype(F32).reshape(CHUNKS * 16, 128)
    half4 = lax.broadcasted_iota(jnp.int32, (4, 128), 1) < 64
    for quad in range(QUADS):
        for two in range(2):
            base = (quad * 2 + two) * 9

            def piece(tile, odd):
                return cf[pl.ds((quad * TILES + tile) * 16 + (2 * two + odd) * 4, 4), :]

            parts = (
                [piece(tile, 0) for tile in range(4)]
                + [jnp.where(half4, piece(4, 0), piece(0, 1))]
                + [piece(tile, 1) for tile in range(1, 5)]
            )
            for k, part in enumerate(parts):
                cout[:, (base + k) * 128 : (base + k + 1) * 128] = part.astype(BF16)
    last = pltpu.make_async_copy(cout, cache, c_sem)
    last.start()

    @pl.when(middle)
    def _():
        done(xs.at[pl.ds(0, CHUNKS - 1)], send1)
        done(os.at[pl.ds(0, 127)], send2)

    @pl.when(jnp.logical_not(middle))
    def _():
        done(xs, send1)

    @pl.when(has_right)
    def _():
        lat_copy.wait_send()
        rope_copy.wait_send()

    for i in range(STEPS):
        result(i).wait()
    last.wait()


def on_device(query, latent_raw, rope_raw, kv_gain, w_uk, w_uv, request_lengths, page_owner, page_slot):
    hbm = pl.BlockSpec(memory_space=pltpu.HBM)
    dma = pltpu.SemaphoreType.DMA

    def b16(*shape):
        return pltpu.VMEM(shape, BF16)

    def f32(*shape):
        return pltpu.VMEM(shape, F32)

    return pl.pallas_call(
        kernel,
        out_shape=(
            jax.ShapeDtypeStruct((TOK, HEADS * 128), BF16),
            jax.ShapeDtypeStruct((4, PAGE_W), BF16),
        ),
        in_specs=[hbm] * 10,
        out_specs=(hbm, hbm),
        scratch_shapes=[
            pltpu.SMEM((1, 32), jnp.int32),
            f32(1, LATENT),
            b16(TOK, LATENT),
            b16(64, TOK),
            b16(384, 256),
            pltpu.VMEM((1, 256), jnp.int32),
            pltpu.VMEM((1, 256), jnp.int32),
            b16(STEPS, TOK, QWIDE),
            b16(STEPS, LATENT, WIDE),
            b16(STEPS, LATENT, WIDE),
            b16(STEPS, TOK, WIDE),
            b16(2 * TOK, LATENT),
            b16(2 * TOK, TOK),
            f32(TOK, TOK),
            f32(TOK, TOK),
            f32(TOK, TOK),
            b16(TOK, TOK),
            b16(TOK, TOK),
            f32(TILES, TOK, 128),
            b16(CHUNKS, 8, 128),
            b16(128, 8, 128),
            f32(1024, 128),
            f32(2048, 128),
            b16(128, 16, 128),
            b16(CHUNKS, 16, 128),
            f32(CHUNKS * 16, 128),
            b16(4, PAGE_W),
            b16(512, 256),
            b16(HEADS_STEP, TOK, 256),
            b16(HEADS_STEP, TOK, 256),
            b16(HEADS_STEP, 256, 256),
            b16(HEADS_STEP, 256, 256),
            b16(HEADS_STEP, 256, 256),
            b16(HEADS_STEP, 256, 256),
            f32(HEADS_STEP, TOK, TOK),
            b16(HEADS_STEP, TOK, 256),
            dma((7,)),
            dma((STEPS,)),
            dma((STEPS,)),
            dma((STEPS,)),
            dma((STEPS,)),
            dma((2,)),
            dma((2,)),
            dma,
            dma,
            dma,
            dma,
            dma,
        ],
        compiler_params=pltpu.CompilerParams(
            collective_id=0, has_side_effects=True, vmem_limit_bytes=56 * 2**20
        ),
        name="prefill_and_pages",
    )(
        request_lengths,
        kv_gain.reshape(1, LATENT),
        latent_raw,
        rope_raw.T,
        jnp.asarray(trig_table()),
        page_owner.reshape(1, 256),
        page_slot.reshape(1, 256),
        query,
        w_uk,
        w_uv,
    )


def solution(mesh):
    rows = P(("group", "seq"), None)
    return jax.shard_map(
        on_device,
        mesh=mesh,
        in_specs=(rows, rows, rows, P(), P(), P(), P("group", None), P(), P()),
        out_specs=(rows, rows),
        check_vma=False,
    )
```

```python
import functools

import jax
import jax.numpy as jnp
import numpy as np
from jax import lax
from jax.experimental import pallas as pl
from jax.experimental.pallas import tpu as pltpu
from jax.sharding import PartitionSpec as P
import ml_dtypes

MESH = pl.DeviceIdType.MESH
F32 = jnp.float32
BF16 = jnp.bfloat16
TOK = 128
HEADS = 64
LATENT = 512
QUADS = 16
TILES = 5
CHUNKS = QUADS * TILES
STEPS = 8
WIDE = 1024
QWIDE = 1536
HEADS_STEP = 8
MIDS = 10
PAGE_W = 36864
SCALE = float(1.0 / 192.0**0.5 * np.log2(np.e))


def trig_table():
    freqs = (10000.0 ** (-np.arange(32, dtype=np.float64) / 32.0)).astype(np.float32)
    angle = np.arange(TOK, dtype=np.float32)[:, None] * freqs[None, :]
    cosine = np.cos(angle.astype(np.float64)).astype(np.float32)
    sine = np.sin(angle.astype(np.float64)).astype(np.float32)
    full = np.concatenate([cosine] * 4 + [-sine, sine, -sine, sine], axis=1)
    parts = []
    for _ in range(3):
        part = full.astype(ml_dtypes.bfloat16)
        parts.append(part)
        full = full - part.astype(np.float32)
    return np.concatenate(parts, axis=0)


def remote(src, dst, send, recv, device):
    return pltpu.make_async_remote_copy(
        src_ref=src, dst_ref=dst, send_sem=send, recv_sem=recv, device_id=device, device_id_type=MESH
    )


def done(ref, sem):
    pltpu.make_async_copy(ref, ref, sem).wait()


def rotated(x, cosine, sine, low):
    partner = jnp.where(low, pltpu.roll(x, 96, 1), pltpu.roll(x, 32, 1))
    return x * cosine + partner * sine


def kernel(
    lengths, gain, latent_raw, rope_raw, trig, owner, slot, query, w_uk, w_uv,
    out, cache,
    lengths_s, gain_v, latent_v, rope_v, trig_v, owner_v, slot_v,
    qv, kv, vv, lat2, kr2, cos_v, sin_v, bias, low_m, up_m, ypage, xs, rs, rf, of, os, cb, cf, onehot,
    left0, left1, right0, right1, value0, value1, score_v, prob_v,
    in_sem, q_sem, k_sem, v_sem, send_n, recv_n, send1, recv1, send2, recv2,
):
    lefts, rights, valued = (left0, left1), (right0, right1), (value0, value1)
    g, s = lax.axis_index("group"), lax.axis_index("seq")
    me = g * 16 + s
    middle = s < MIDS
    my_chunk = jnp.where(middle, s * 8 + g, 0)
    has_left, has_right = s > 0, s < 15
    early = s < 8

    small = [
        pltpu.make_async_copy(src, dst, in_sem.at[i])
        for i, (src, dst) in enumerate(
            (
                (latent_raw, latent_v),
                (gain, gain_v),
                (lengths, lengths_s),
                (rope_raw, rope_v),
                (trig, trig_v),
                (owner, owner_v),
                (slot, slot_v),
            )
        )
    ]
    for copy in small:
        copy.start()

    def fetches(i):
        return (
            pltpu.make_async_copy(query.at[:, pl.ds(i * QWIDE, QWIDE)], qv.at[i], q_sem.at[i]),
            pltpu.make_async_copy(w_uk.at[:, pl.ds(i * WIDE, WIDE)], kv.at[i], k_sem.at[i]),
            pltpu.make_async_copy(w_uv.at[:, pl.ds(i * WIDE, WIDE)], vv.at[i], v_sem.at[i]),
        )

    def fetched(i):
        for fetch in fetches(i):
            fetch.wait()

    barrier = pltpu.get_barrier_semaphore()

    def greet(device):
        pl.semaphore_signal(barrier, inc=1, device_id=device, device_id_type=MESH)

    @pl.when(middle)
    def _():
        for b in range(16):
            for a in range(8):
                pl.when(me != a * 16 + b)(functools.partial(greet, (a, b)))

    @pl.when(has_left)
    def _():
        greet((g, s - 1))

    for i in range(STEPS):
        for fetch in fetches(i):
            fetch.start()

    row = lax.broadcasted_iota(jnp.int32, (TOK, TOK), 0)
    col = lax.broadcasted_iota(jnp.int32, (TOK, TOK), 1)
    low = col % 64 < 32
    half = col < 64
    odd = row % 2 == 1
    upper = lax.broadcasted_iota(jnp.int32, (8, 128), 0) < 4

    for copy in small[:2]:
        copy.wait()
    source = latent_v[...].astype(F32)
    norm = lax.rsqrt(jnp.mean(source * source, axis=1, keepdims=True) + 1e-06)
    latent = (source * norm * gain_v[...]).astype(BF16)
    lat2[TOK:, :] = latent

    wide = latent.astype(F32)
    plain = [wide[:, i * 128 : (i + 1) * 128] for i in range(4)]
    turned = [pltpu.roll(x, 64, 1) for x in plain]
    moved = [turned[0]] + [jnp.where(half, turned[i - 1], turned[i]) for i in range(1, 4)]

    def chunked(tile):
        for octet in range(8):
            first = ypage[tile, octet * 8 : octet * 8 + 8, :]
            second = ypage[tile, 64 + octet * 8 : 64 + octet * 8 + 8, :]
            xs[tile * QUADS + 2 * octet] = jnp.where(upper, first, pltpu.roll(second, 4, 0)).astype(BF16)
            xs[tile * QUADS + 2 * octet + 1] = jnp.where(upper, pltpu.roll(first, 4, 0), second).astype(BF16)

    for tile, (a, b) in enumerate(zip(plain, moved)):
        ypage[tile] = jnp.where(odd, b, a)
    for tile in range(4):
        chunked(tile)

    pl.semaphore_wait(barrier, 8 * MIDS - jnp.where(middle, 1, 0) + jnp.where(has_right, 1, 0))

    lat_copy = remote(lat2.at[pl.ds(TOK, TOK)], lat2.at[pl.ds(0, TOK)], send_n.at[0], recv_n.at[0], (g, s + 1))
    rope_copy = remote(kr2.at[pl.ds(TOK, TOK)], kr2.at[pl.ds(0, TOK)], send_n.at[1], recv_n.at[1], (g, s + 1))
    pl.when(has_right & early)(lat_copy.start)

    def first_hop(b):
        for a in range(8):
            copy = remote(xs.at[b * 8 + a], rs.at[me], send1, recv1, (a, b))
            pl.when(me != a * 16 + b)(copy.start)

    for b in range(8):
        first_hop(b)

    for copy in small[2:]:
        copy.wait()
    index = lax.broadcasted_iota(jnp.int32, (8, TOK), 1) + s * TOK
    begin = jnp.zeros((8, TOK), jnp.int32)
    start = jnp.int32(0)
    for r in range(32):
        begin = jnp.where(index >= start, start, begin)
        start = start + lengths_s[0, r]
    pos = (index - begin).astype(F32)
    pos = jnp.concatenate([pos] * 16, axis=0).T.astype(jnp.int32)
    hot = (col == pos).astype(F32).astype(BF16)
    angles = jnp.dot(jnp.concatenate([hot, hot, hot], axis=1), trig_v[...], preferred_element_type=F32)
    cosine, sine = angles[:, :TOK], angles[:, TOK:]
    rope = rope_v[...].astype(F32)
    rope = jnp.concatenate([rope, rope], axis=0).T
    key_rope = rotated(rope, cosine, sine, low).astype(BF16)
    kr2[TOK:, :] = key_rope
    tail = key_rope.astype(F32)
    last_lanes = pltpu.roll(lat2[TOK:, 384:].astype(F32), 64, 1)
    ypage[4] = jnp.where(odd, jnp.where(half, last_lanes, tail), tail)
    chunked(4)
    pl.when(has_right)(rope_copy.start)
    for b in range(8, MIDS):
        first_hop(b)
    pl.when(has_right & jnp.logical_not(early))(lat_copy.start)

    cos_v[...] = cosine
    sin_v[...] = sine
    bias[...] = jnp.where((row - col + TOK) % TOK <= pos, 0.0, -1e30)
    low_m[...] = jnp.where(col <= row, 1.0, 0.0).astype(BF16)
    up_m[...] = jnp.where(col <= row, 0.0, 1.0).astype(BF16)
    for value in valued:
        value[:, :, TOK:] = jnp.ones((HEADS_STEP, 2 * TOK, TOK), BF16)

    @pl.when(middle)
    def _():
        rs[me] = xs[my_chunk]
        want = slot_v[...] * 128 + owner_v[...]
        onehot[...] = (lax.broadcasted_iota(jnp.int32, (512, 256), 0) == want).astype(F32).astype(BF16)

    @pl.when(has_left)
    def _():
        done(lat2.at[pl.ds(0, TOK)], recv_n.at[0])
        done(kr2.at[pl.ds(0, TOK)], recv_n.at[1])

    @pl.when(s == 0)
    def _():
        lat2[:TOK, :] = jnp.zeros((TOK, LATENT), BF16)
        kr2[:TOK, :] = jnp.zeros((TOK, TOK), BF16)

    ropes = kr2[...].astype(F32).T
    first_half = lax.broadcasted_iota(jnp.int32, (TOK, 2 * TOK), 0) < 64
    for one in range(2):
        masked = jnp.where(first_half if one == 0 else ~first_half, ropes, 0.0).astype(BF16)
        for right in rights:
            for pair in range(HEADS_STEP // 2):
                right[2 * pair + one, TOK:, :] = masked

    def prepare(i, b, piece):
        pair = piece // 2
        columns = slice(pair * 256, pair * 256 + 256)
        if piece % 2:
            values = jnp.dot(lat2[...], vv[i, :, columns], preferred_element_type=F32).astype(BF16)
            for one in range(2):
                valued[b][2 * pair + one, :, :TOK] = values[:, one * 128 : one * 128 + 128]
            return
        keys = jnp.dot(lat2[...], kv[i, :, columns], preferred_element_type=F32).astype(BF16)
        for one in range(2):
            rights[b][2 * pair + one, :TOK, :] = keys[:, one * 128 : one * 128 + 128].T
        col = lax.broadcasted_iota(jnp.int32, (TOK, TOK), 1)
        half = col < 64
        low = col % 64 < 32
        t0, t1, t2 = [qv[i, :, pl.ds(pair * 384 + t * 128, 128)] for t in range(3)]
        ropes = jnp.where(half, t1, t2).astype(F32)
        turn = rotated(ropes, cos_v[...], sin_v[...], low).astype(BF16)
        second = pltpu.roll(jnp.where(half, t2, t1).astype(F32), 64, 1).astype(BF16)
        for one, nope in enumerate((t0, second)):
            lefts[b][2 * pair + one, :, :TOK] = nope
            lefts[b][2 * pair + one, :, TOK:] = turn

    def scored(b, h):
        row = lax.broadcasted_iota(jnp.int32, (TOK, TOK), 0)
        col = lax.broadcasted_iota(jnp.int32, (TOK, TOK), 1)
        score = jnp.dot(lefts[b][h], rights[b][h], preferred_element_type=F32)
        score_v[h] = jnp.where(col <= row, score[:, TOK:], score[:, :TOK]) + bias[...]

    def softened(h):
        score = score_v[h]
        top = jnp.max(score, axis=1, keepdims=True)
        weight = jnp.exp2((score - top) * SCALE).astype(BF16)
        prob_v[h, :, :TOK] = weight * up_m[...]
        prob_v[h, :, TOK:] = weight * low_m[...]

    def summed(i, b, h):
        got = jnp.dot(prob_v[h], valued[b][h], preferred_element_type=F32)
        out[:, pl.ds(i * WIDE + h * 128, 128)] = (got[:, :TOK] * (1.0 / got[:, TOK:])).astype(BF16)

    def step(i, b, more=True):
        if b == 0:
            fetched(i + 1)
        elif more:
            pl.when(i + 1 < STEPS)(lambda: fetched(i + 1))
        for h in range(HEADS_STEP + 4):
            if h < HEADS_STEP:
                scored(b, h)
            if 0 <= h - 2 < HEADS_STEP:
                softened(h - 2)
            if 0 <= h - 4 < HEADS_STEP:
                summed(i, b, h - 4)
            if more and 0 <= h - 2 < HEADS_STEP:
                prepare(i + 1, 1 - b, h - 2)

    fetched(0)
    for piece in range(HEADS_STEP):
        prepare(0, 0, piece)

    @pl.loop(0, STEPS // 2 - 1)
    def _(j):
        @pl.when((j == 1) & middle)
        def _():
            done(rs.at[pl.ds(0, 127)], recv1)
            rf[...] = rs[...].astype(F32).reshape(1024, 128)
            pages = jnp.concatenate([rf[pl.ds(t, 256, stride=4), :].astype(BF16) for t in range(4)], axis=1)
            picked = jnp.dot(onehot[...], pages, preferred_element_type=F32)
            for t in range(4):
                for k in range(4):
                    of[pl.ds(t * 4 + k, 128, stride=16), :] = picked[
                        k * 128 : (k + 1) * 128, t * 128 : (t + 1) * 128
                    ]
            os[...] = of[...].reshape(128, 16, 128).astype(BF16)
            cb[my_chunk] = os[me]
            z, x = s // 4, s % 4
            for zh in range(2):
                for xh in range(2):
                    for dg in range(8):
                        a = lax.rem(g + dg, 8)
                        for dz in range(2):
                            for dx in range(2):
                                b = (zh * 2 + lax.rem(z + dz, 2)) * 4 + xh * 2 + lax.rem(x + dx, 2)
                                copy = remote(os.at[a * 16 + b], cb.at[my_chunk], send2, recv2, (a, b))
                                if dg + dz + dx:
                                    copy.start()
                                else:
                                    pl.when((z // 2 != zh) | (x // 2 != xh))(copy.start)

        for b in range(2):
            step(2 * j + b, b)

    step(STEPS - 2, 0)

    @pl.when(middle)
    def _():
        done(cb.at[pl.ds(0, CHUNKS - 1)], recv2)

    @pl.when(jnp.logical_not(middle))
    def _():
        done(cb, recv2)

    cf[...] = cb[...].astype(F32).reshape(CHUNKS * 16, 128)
    half4 = lax.broadcasted_iota(jnp.int32, (4, 128), 1) < 64
    for quad in range(QUADS):
        for two in range(2):
            base = (quad * 2 + two) * 9

            def piece(tile, odd):
                return cf[pl.ds((tile * QUADS + quad) * 16 + (2 * two + odd) * 4, 4), :]

            parts = (
                [piece(tile, 0) for tile in range(4)]
                + [jnp.where(half4, piece(4, 0), piece(0, 1))]
                + [piece(tile, 1) for tile in range(1, 5)]
            )
            for k, part in enumerate(parts):
                cache[:, (base + k) * 128 : (base + k + 1) * 128] = part.astype(BF16)

    step(STEPS - 1, 1, more=False)

    @pl.when(middle)
    def _():
        done(xs.at[pl.ds(0, CHUNKS - 1)], send1)
        done(os.at[pl.ds(0, 127)], send2)

    @pl.when(jnp.logical_not(middle))
    def _():
        done(xs, send1)

    @pl.when(has_right)
    def _():
        lat_copy.wait_send()
        rope_copy.wait_send()


def written(attended, cache, attended_out, cache_out, sem):
    copies = [pltpu.make_async_copy(cache, cache_out, sem.at[4])]
    for i in range(4):
        rows = pl.ds(i * 32, 32)
        copies.append(pltpu.make_async_copy(attended.at[rows], attended_out.at[rows], sem.at[i]))
    for copy in copies:
        copy.start()
    for copy in copies:
        copy.wait()


def on_device(query, latent_raw, rope_raw, kv_gain, w_uk, w_uv, request_lengths, page_owner, page_slot):
    hbm = pl.BlockSpec(memory_space=pltpu.HBM)
    dma = pltpu.SemaphoreType.DMA

    def b16(*shape):
        return pltpu.VMEM(shape, BF16)

    def f32(*shape):
        return pltpu.VMEM(shape, F32)

    vmem = pl.BlockSpec(memory_space=pltpu.VMEM)
    shapes = (
        jax.ShapeDtypeStruct((TOK, HEADS * 128), BF16),
        jax.ShapeDtypeStruct((4, PAGE_W), BF16),
    )
    attended, cache = pl.pallas_call(
        kernel,
        out_shape=(pltpu.VMEM(shapes[0].shape, BF16), pltpu.VMEM(shapes[1].shape, BF16)),
        in_specs=[hbm] * 10,
        out_specs=(vmem, vmem),
        scratch_shapes=[
            pltpu.SMEM((1, 32), jnp.int32),
            f32(1, LATENT),
            b16(TOK, LATENT),
            b16(64, TOK),
            b16(384, 256),
            pltpu.VMEM((1, 256), jnp.int32),
            pltpu.VMEM((1, 256), jnp.int32),
            b16(STEPS, TOK, QWIDE),
            b16(STEPS, LATENT, WIDE),
            b16(STEPS, LATENT, WIDE),
            b16(2 * TOK, LATENT),
            b16(2 * TOK, TOK),
            f32(TOK, TOK),
            f32(TOK, TOK),
            f32(TOK, TOK),
            b16(TOK, TOK),
            b16(TOK, TOK),
            f32(TILES, TOK, 128),
            b16(CHUNKS, 8, 128),
            b16(128, 8, 128),
            f32(1024, 128),
            f32(2048, 128),
            b16(128, 16, 128),
            b16(CHUNKS, 16, 128),
            f32(CHUNKS * 16, 128),
            b16(512, 256),
            b16(HEADS_STEP, TOK, 256),
            b16(HEADS_STEP, TOK, 256),
            b16(HEADS_STEP, 256, 256),
            b16(HEADS_STEP, 256, 256),
            b16(HEADS_STEP, 256, 256),
            b16(HEADS_STEP, 256, 256),
            f32(HEADS_STEP, TOK, TOK),
            b16(HEADS_STEP, TOK, 256),
            dma((7,)),
            dma((STEPS,)),
            dma((STEPS,)),
            dma((STEPS,)),
            dma((2,)),
            dma((2,)),
            dma,
            dma,
            dma,
            dma,
        ],
        compiler_params=pltpu.CompilerParams(
            collective_id=0, has_side_effects=True, vmem_limit_bytes=44 * 2**20
        ),
        name="prefill_and_pages",
    )(
        *(
            pltpu.with_memory_space_constraint(x, pltpu.HBM)
            for x in (
                request_lengths,
                kv_gain.reshape(1, LATENT),
                latent_raw,
                rope_raw.T,
                jnp.asarray(trig_table()),
                page_owner.reshape(1, 256),
                page_slot.reshape(1, 256),
                query,
                w_uk,
                w_uv,
            )
        )
    )
    return pl.pallas_call(
        written,
        out_shape=shapes,
        in_specs=[vmem] * 2,
        out_specs=(hbm, hbm),
        scratch_shapes=[dma((5,))],
        name="results_out",
    )(attended, cache)


def solution(mesh):
    rows = P(("group", "seq"), None)
    return jax.shard_map(
        on_device,
        mesh=mesh,
        in_specs=(rows, rows, rows, P(), P(), P(), P("group", None), P(), P()),
        out_specs=(rows, rows),
        check_vma=False,
    )
```

```python
import functools

import jax
import jax.numpy as jnp
import numpy as np
from jax import lax
from jax.experimental import pallas as pl
from jax.experimental.pallas import tpu as pltpu
from jax.sharding import PartitionSpec as P
import ml_dtypes

MESH = pl.DeviceIdType.MESH
F32 = jnp.float32
BF16 = jnp.bfloat16
TOK = 128
HEADS = 64
LATENT = 512
QUADS = 16
TILES = 5
CHUNKS = QUADS * TILES
STEPS = 8
WIDE = 1024
QWIDE = 1536
HEADS_STEP = 8
MIDS = 10
PAGE_W = 36864
SCALE = float(1.0 / 192.0**0.5 * np.log2(np.e))


def trig_table():
    freqs = (10000.0 ** (-np.arange(32, dtype=np.float64) / 32.0)).astype(np.float32)
    angle = np.arange(TOK, dtype=np.float32)[:, None] * freqs[None, :]
    cosine = np.cos(angle.astype(np.float64)).astype(np.float32)
    sine = np.sin(angle.astype(np.float64)).astype(np.float32)
    full = np.concatenate([cosine] * 4 + [-sine, sine, -sine, sine], axis=1)
    parts = []
    for _ in range(3):
        part = full.astype(ml_dtypes.bfloat16)
        parts.append(part)
        full = full - part.astype(np.float32)
    return np.concatenate(parts, axis=0)


def remote(src, dst, send, recv, device):
    return pltpu.make_async_remote_copy(
        src_ref=src, dst_ref=dst, send_sem=send, recv_sem=recv, device_id=device, device_id_type=MESH
    )


def done(ref, sem):
    pltpu.make_async_copy(ref, ref, sem).wait()


def rotated(x, cosine, sine, low):
    partner = jnp.where(low, pltpu.roll(x, 96, 1), pltpu.roll(x, 32, 1))
    return x * cosine + partner * sine


def kernel(
    lengths, gain, latent_raw, rope_raw, trig, owner, slot, query, w_uk, w_uv,
    out, cache,
    lengths_s, gain_v, latent_v, rope_v, trig_v, owner_v, slot_v,
    qv, kv, vv, lat2, kr2, cos_v, sin_v, bias, low_m, up_m, ypage, xs, rs, rf, of, os, cb, cf, onehot,
    left0, left1, right0, right1, value0, value1, score_v, prob_v,
    in_sem, q_sem, k_sem, v_sem, send_n, recv_n, send1, recv1, send2, recv2,
):
    lefts, rights, valued = (left0, left1), (right0, right1), (value0, value1)
    g, s = lax.axis_index("group"), lax.axis_index("seq")
    me = g * 16 + s
    middle = s < MIDS
    my_chunk = jnp.where(middle, s * 8 + g, 0)
    has_left, has_right = s > 0, s < 15
    early = s < 8

    small = [
        pltpu.make_async_copy(src, dst, in_sem.at[i])
        for i, (src, dst) in enumerate(
            (
                (latent_raw, latent_v),
                (gain, gain_v),
                (lengths, lengths_s),
                (rope_raw, rope_v),
                (trig, trig_v),
                (owner, owner_v),
                (slot, slot_v),
            )
        )
    ]
    for copy in small:
        copy.start()

    def fetches(i):
        return (
            pltpu.make_async_copy(query.at[:, pl.ds(i * QWIDE, QWIDE)], qv.at[i], q_sem.at[i]),
            pltpu.make_async_copy(w_uk.at[:, pl.ds(i * WIDE, WIDE)], kv.at[i], k_sem.at[i]),
            pltpu.make_async_copy(w_uv.at[:, pl.ds(i * WIDE, WIDE)], vv.at[i], v_sem.at[i]),
        )

    def fetched(i):
        for fetch in fetches(i):
            fetch.wait()

    barrier = pltpu.get_barrier_semaphore()

    def greet(device):
        pl.semaphore_signal(barrier, inc=1, device_id=device, device_id_type=MESH)

    @pl.when(middle)
    def _():
        for b in range(16):
            for a in range(8):
                pl.when(me != a * 16 + b)(functools.partial(greet, (a, b)))

    @pl.when(has_left)
    def _():
        greet((g, s - 1))

    for i in range(STEPS):
        for fetch in fetches(i):
            fetch.start()

    row = lax.broadcasted_iota(jnp.int32, (TOK, TOK), 0)
    col = lax.broadcasted_iota(jnp.int32, (TOK, TOK), 1)
    low = col % 64 < 32
    half = col < 64
    odd = row % 2 == 1
    upper = lax.broadcasted_iota(jnp.int32, (8, 128), 0) < 4

    for copy in small[:2]:
        copy.wait()
    source = latent_v[...].astype(F32)
    norm = lax.rsqrt(jnp.mean(source * source, axis=1, keepdims=True) + 1e-06)
    latent = (source * norm * gain_v[...]).astype(BF16)
    lat2[TOK:, :] = latent

    wide = latent.astype(F32)
    plain = [wide[:, i * 128 : (i + 1) * 128] for i in range(4)]
    turned = [pltpu.roll(x, 64, 1) for x in plain]
    moved = [turned[0]] + [jnp.where(half, turned[i - 1], turned[i]) for i in range(1, 4)]

    def chunked(tile):
        for octet in range(8):
            first = ypage[tile, octet * 8 : octet * 8 + 8, :]
            second = ypage[tile, 64 + octet * 8 : 64 + octet * 8 + 8, :]
            xs[tile * QUADS + 2 * octet] = jnp.where(upper, first, pltpu.roll(second, 4, 0)).astype(BF16)
            xs[tile * QUADS + 2 * octet + 1] = jnp.where(upper, pltpu.roll(first, 4, 0), second).astype(BF16)

    for tile, (a, b) in enumerate(zip(plain, moved)):
        ypage[tile] = jnp.where(odd, b, a)
    for tile in range(4):
        chunked(tile)

    pl.semaphore_wait(barrier, 8 * MIDS - jnp.where(middle, 1, 0) + jnp.where(has_right, 1, 0))

    lat_copy = remote(lat2.at[pl.ds(TOK, TOK)], lat2.at[pl.ds(0, TOK)], send_n.at[0], recv_n.at[0], (g, s + 1))
    rope_copy = remote(kr2.at[pl.ds(TOK, TOK)], kr2.at[pl.ds(0, TOK)], send_n.at[1], recv_n.at[1], (g, s + 1))
    pl.when(has_right & early)(lat_copy.start)

    def first_hop(b):
        for a in range(8):
            copy = remote(xs.at[b * 8 + a], rs.at[me], send1, recv1, (a, b))
            pl.when(me != a * 16 + b)(copy.start)

    for b in range(8):
        first_hop(b)

    for copy in small[2:]:
        copy.wait()
    index = lax.broadcasted_iota(jnp.int32, (8, TOK), 1) + s * TOK
    begin = jnp.zeros((8, TOK), jnp.int32)
    start = jnp.int32(0)
    for r in range(32):
        begin = jnp.where(index >= start, start, begin)
        start = start + lengths_s[0, r]
    pos = (index - begin).astype(F32)
    pos = jnp.concatenate([pos] * 16, axis=0).T.astype(jnp.int32)
    hot = (col == pos).astype(F32).astype(BF16)
    angles = jnp.dot(jnp.concatenate([hot, hot, hot], axis=1), trig_v[...], preferred_element_type=F32)
    cosine, sine = angles[:, :TOK], angles[:, TOK:]
    rope = rope_v[...].astype(F32)
    rope = jnp.concatenate([rope, rope], axis=0).T
    key_rope = rotated(rope, cosine, sine, low).astype(BF16)
    kr2[TOK:, :] = key_rope
    tail = key_rope.astype(F32)
    last_lanes = pltpu.roll(lat2[TOK:, 384:].astype(F32), 64, 1)
    ypage[4] = jnp.where(odd, jnp.where(half, last_lanes, tail), tail)
    chunked(4)
    pl.when(has_right)(rope_copy.start)
    for b in range(8, MIDS):
        first_hop(b)
    pl.when(has_right & jnp.logical_not(early))(lat_copy.start)

    cos_v[...] = cosine
    sin_v[...] = sine
    bias[...] = jnp.where((row - col + TOK) % TOK <= pos, 0.0, -1e30)
    low_m[...] = jnp.where(col <= row, 1.0, 0.0).astype(BF16)
    up_m[...] = jnp.where(col <= row, 0.0, 1.0).astype(BF16)
    for value in valued:
        value[:, :, TOK:] = jnp.ones((HEADS_STEP, 2 * TOK, TOK), BF16)

    @pl.when(middle)
    def _():
        rs[me] = xs[my_chunk]
        want = slot_v[...] * 128 + owner_v[...]
        onehot[...] = (lax.broadcasted_iota(jnp.int32, (512, 256), 0) == want).astype(F32).astype(BF16)

    @pl.when(has_left)
    def _():
        done(lat2.at[pl.ds(0, TOK)], recv_n.at[0])
        done(kr2.at[pl.ds(0, TOK)], recv_n.at[1])

    @pl.when(s == 0)
    def _():
        lat2[:TOK, :] = jnp.zeros((TOK, LATENT), BF16)
        kr2[:TOK, :] = jnp.zeros((TOK, TOK), BF16)

    ropes = kr2[...].astype(F32).T
    first_half = lax.broadcasted_iota(jnp.int32, (TOK, 2 * TOK), 0) < 64
    for one in range(2):
        masked = jnp.where(first_half if one == 0 else ~first_half, ropes, 0.0).astype(BF16)
        for right in rights:
            for pair in range(HEADS_STEP // 2):
                right[2 * pair + one, TOK:, :] = masked

    def prepare(i, b, piece):
        pair = piece // 2
        columns = slice(pair * 256, pair * 256 + 256)
        if piece % 2:
            values = jnp.dot(lat2[...], vv[i, :, columns], preferred_element_type=F32).astype(BF16)
            for one in range(2):
                valued[b][2 * pair + one, :, :TOK] = values[:, one * 128 : one * 128 + 128]
            return
        keys = jnp.dot(lat2[...], kv[i, :, columns], preferred_element_type=F32).astype(BF16)
        for one in range(2):
            rights[b][2 * pair + one, :TOK, :] = keys[:, one * 128 : one * 128 + 128].T
        col = lax.broadcasted_iota(jnp.int32, (TOK, TOK), 1)
        half = col < 64
        low = col % 64 < 32
        t0, t1, t2 = [qv[i, :, pl.ds(pair * 384 + t * 128, 128)] for t in range(3)]
        ropes = jnp.where(half, t1, t2).astype(F32)
        turn = rotated(ropes, cos_v[...], sin_v[...], low).astype(BF16)
        second = pltpu.roll(jnp.where(half, t2, t1).astype(F32), 64, 1).astype(BF16)
        for one, nope in enumerate((t0, second)):
            lefts[b][2 * pair + one, :, :TOK] = nope
            lefts[b][2 * pair + one, :, TOK:] = turn

    def scored(b, h):
        row = lax.broadcasted_iota(jnp.int32, (TOK, TOK), 0)
        col = lax.broadcasted_iota(jnp.int32, (TOK, TOK), 1)
        score = jnp.dot(lefts[b][h], rights[b][h], preferred_element_type=F32)
        score_v[h] = jnp.where(col <= row, score[:, TOK:], score[:, :TOK]) + bias[...]

    def softened(h):
        score = score_v[h]
        top = jnp.max(score, axis=1, keepdims=True)
        weight = jnp.exp2((score - top) * SCALE).astype(BF16)
        prob_v[h, :, :TOK] = weight * up_m[...]
        prob_v[h, :, TOK:] = weight * low_m[...]

    def summed(i, b, h):
        got = jnp.dot(prob_v[h], valued[b][h], preferred_element_type=F32)
        out[:, pl.ds(i * WIDE + h * 128, 128)] = (got[:, :TOK] * (1.0 / got[:, TOK:])).astype(BF16)

    def step(i, b, more=True):
        if b == 0:
            fetched(i + 1)
        elif more:
            pl.when(i + 1 < STEPS)(lambda: fetched(i + 1))
        for h in range(HEADS_STEP + 4):
            if h < HEADS_STEP:
                scored(b, h)
            if 0 <= h - 2 < HEADS_STEP:
                softened(h - 2)
            if 0 <= h - 4 < HEADS_STEP:
                summed(i, b, h - 4)
            if more and 0 <= h - 2 < HEADS_STEP:
                prepare(i + 1, 1 - b, h - 2)

    fetched(0)
    for piece in range(HEADS_STEP):
        prepare(0, 0, piece)

    @pl.loop(0, STEPS // 2 - 1)
    def _(j):
        @pl.when((j == 1) & middle)
        def _():
            done(rs.at[pl.ds(0, 127)], recv1)
            rf[...] = rs[...].astype(F32).reshape(1024, 128)
            pages = jnp.concatenate([rf[pl.ds(t, 256, stride=4), :].astype(BF16) for t in range(4)], axis=1)
            picked = jnp.dot(onehot[...], pages, preferred_element_type=F32)
            for t in range(4):
                for k in range(4):
                    of[pl.ds(t * 4 + k, 128, stride=16), :] = picked[
                        k * 128 : (k + 1) * 128, t * 128 : (t + 1) * 128
                    ]
            os[...] = of[...].reshape(128, 16, 128).astype(BF16)
            cb[my_chunk] = os[me]
            z, x = s // 4, s % 4
            for zh in range(2):
                for xh in range(2):
                    for dg in range(8):
                        a = lax.rem(g + dg, 8)
                        for dz in range(2):
                            for dx in range(2):
                                b = (zh * 2 + lax.rem(z + dz, 2)) * 4 + xh * 2 + lax.rem(x + dx, 2)
                                copy = remote(os.at[a * 16 + b], cb.at[my_chunk], send2, recv2, (a, b))
                                if dg + dz + dx:
                                    copy.start()
                                else:
                                    pl.when((z // 2 != zh) | (x // 2 != xh))(copy.start)

        for b in range(2):
            step(2 * j + b, b)

    step(STEPS - 2, 0)

    @pl.when(middle)
    def _():
        done(cb.at[pl.ds(0, CHUNKS - 1)], recv2)

    @pl.when(jnp.logical_not(middle))
    def _():
        done(cb, recv2)

    cf[...] = cb[...].astype(F32).reshape(CHUNKS * 16, 128)
    half4 = lax.broadcasted_iota(jnp.int32, (4, 128), 1) < 64
    for quad in range(QUADS):
        for two in range(2):
            base = (quad * 2 + two) * 9

            def piece(tile, odd):
                return cf[pl.ds((tile * QUADS + quad) * 16 + (2 * two + odd) * 4, 4), :]

            parts = (
                [piece(tile, 0) for tile in range(4)]
                + [jnp.where(half4, piece(4, 0), piece(0, 1))]
                + [piece(tile, 1) for tile in range(1, 5)]
            )
            for k, part in enumerate(parts):
                cache[:, (base + k) * 128 : (base + k + 1) * 128] = part.astype(BF16)

    step(STEPS - 1, 1, more=False)

    @pl.when(middle)
    def _():
        done(xs.at[pl.ds(0, CHUNKS - 1)], send1)
        done(os.at[pl.ds(0, 127)], send2)

    @pl.when(jnp.logical_not(middle))
    def _():
        done(xs, send1)

    @pl.when(has_right)
    def _():
        lat_copy.wait_send()
        rope_copy.wait_send()


def written(attended, cache, attended_out, cache_out, sem):
    copies = [pltpu.make_async_copy(cache, cache_out, sem.at[4])]
    for i in range(4):
        rows = pl.ds(i * 32, 32)
        copies.append(pltpu.make_async_copy(attended.at[rows], attended_out.at[rows], sem.at[i]))
    for copy in copies:
        copy.start()
    for copy in copies:
        copy.wait()


def on_device(query, latent_raw, rope_raw, kv_gain, w_uk, w_uv, request_lengths, page_owner, page_slot):
    hbm = pl.BlockSpec(memory_space=pltpu.HBM)
    dma = pltpu.SemaphoreType.DMA

    def b16(*shape):
        return pltpu.VMEM(shape, BF16)

    def f32(*shape):
        return pltpu.VMEM(shape, F32)

    vmem = pl.BlockSpec(memory_space=pltpu.VMEM)
    shapes = (
        jax.ShapeDtypeStruct((TOK, HEADS * 128), BF16),
        jax.ShapeDtypeStruct((4, PAGE_W), BF16),
    )
    attended, cache = pl.pallas_call(
        kernel,
        out_shape=(pltpu.VMEM(shapes[0].shape, BF16), pltpu.VMEM(shapes[1].shape, BF16)),
        in_specs=[hbm] * 10,
        out_specs=(vmem, vmem),
        scratch_shapes=[
            pltpu.SMEM((1, 32), jnp.int32),
            f32(1, LATENT),
            b16(TOK, LATENT),
            b16(64, TOK),
            b16(384, 256),
            pltpu.VMEM((1, 256), jnp.int32),
            pltpu.VMEM((1, 256), jnp.int32),
            b16(STEPS, TOK, QWIDE),
            b16(STEPS, LATENT, WIDE),
            b16(STEPS, LATENT, WIDE),
            b16(2 * TOK, LATENT),
            b16(2 * TOK, TOK),
            f32(TOK, TOK),
            f32(TOK, TOK),
            f32(TOK, TOK),
            b16(TOK, TOK),
            b16(TOK, TOK),
            f32(TILES, TOK, 128),
            b16(CHUNKS, 8, 128),
            b16(128, 8, 128),
            f32(1024, 128),
            f32(2048, 128),
            b16(128, 16, 128),
            b16(CHUNKS, 16, 128),
            f32(CHUNKS * 16, 128),
            b16(512, 256),
            b16(HEADS_STEP, TOK, 256),
            b16(HEADS_STEP, TOK, 256),
            b16(HEADS_STEP, 256, 256),
            b16(HEADS_STEP, 256, 256),
            b16(HEADS_STEP, 256, 256),
            b16(HEADS_STEP, 256, 256),
            f32(HEADS_STEP, TOK, TOK),
            b16(HEADS_STEP, TOK, 256),
            dma((7,)),
            dma((STEPS,)),
            dma((STEPS,)),
            dma((STEPS,)),
            dma((2,)),
            dma((2,)),
            dma,
            dma,
            dma,
            dma,
        ],
        compiler_params=pltpu.CompilerParams(
            collective_id=0, has_side_effects=True, vmem_limit_bytes=44 * 2**20
        ),
        name="prefill_and_pages",
    )(
        *(
            pltpu.with_memory_space_constraint(x, pltpu.HBM)
            for x in (
                request_lengths,
                kv_gain.reshape(1, LATENT),
                latent_raw,
                rope_raw.T,
                jnp.asarray(trig_table()),
                page_owner.reshape(1, 256),
                page_slot.reshape(1, 256),
                query,
                w_uk,
                w_uv,
            )
        )
    )
    return pl.pallas_call(
        written,
        out_shape=shapes,
        in_specs=[vmem] * 2,
        out_specs=(hbm, hbm),
        scratch_shapes=[dma((5,))],
        name="results_out",
    )(
        pltpu.with_memory_space_constraint(attended, pltpu.VMEM), pltpu.with_memory_space_constraint(cache, pltpu.VMEM)
    )


def solution(mesh):
    rows = P(("group", "seq"), None)
    return jax.shard_map(
        on_device,
        mesh=mesh,
        in_specs=(rows, rows, rows, P(), P(), P(), P("group", None), P(), P()),
        out_specs=(rows, rows),
        check_vma=False,
    )
```

```python
import functools

import jax
import jax.numpy as jnp
import numpy as np
from jax import lax
from jax.experimental import pallas as pl
from jax.experimental.pallas import tpu as pltpu
from jax.sharding import PartitionSpec as P
import ml_dtypes

MESH = pl.DeviceIdType.MESH
F32 = jnp.float32
BF16 = jnp.bfloat16
TOK = 128
HEADS = 64
LATENT = 512
QUADS = 16
TILES = 5
CHUNKS = QUADS * TILES
STEPS = 8
WIDE = 1024
QWIDE = 1536
HEADS_STEP = 8
MIDS = 10
EVENT = 1
PAGE_W = 36864
SCALE = float(1.0 / 192.0**0.5 * np.log2(np.e))


def trig_table():
    freqs = (10000.0 ** (-np.arange(32, dtype=np.float64) / 32.0)).astype(np.float32)
    angle = np.arange(TOK, dtype=np.float32)[:, None] * freqs[None, :]
    cosine = np.cos(angle.astype(np.float64)).astype(np.float32)
    sine = np.sin(angle.astype(np.float64)).astype(np.float32)
    full = np.concatenate([cosine] * 4 + [-sine, sine, -sine, sine], axis=1)
    parts = []
    for _ in range(3):
        part = full.astype(ml_dtypes.bfloat16)
        parts.append(part)
        full = full - part.astype(np.float32)
    return np.concatenate(parts, axis=0)


def remote(src, dst, send, recv, device):
    return pltpu.make_async_remote_copy(
        src_ref=src, dst_ref=dst, send_sem=send, recv_sem=recv, device_id=device, device_id_type=MESH
    )


def done(ref, sem):
    pltpu.make_async_copy(ref, ref, sem).wait()


def rotated(x, cosine, sine, low):
    partner = jnp.where(low, pltpu.roll(x, 96, 1), pltpu.roll(x, 32, 1))
    return x * cosine + partner * sine


def kernel(
    lengths, gain, latent_raw, rope_raw, trig, owner, slot, query, w_uk, w_uv,
    out, chunks,
    lengths_s, gain_v, latent_v, rope_v, trig_v, owner_v, slot_v,
    qv, kv, vv, lat2, kr2, cos_v, sin_v, bias, low_m, up_m, ypage, xs, rs, rf, of, os, cb, onehot,
    left0, left1, right0, right1, value0, value1, score_v, prob_v,
    in_sem, q_sem, k_sem, v_sem, send_n, recv_n, send1, recv1, send2, recv2,
):
    lefts, rights, valued = (left0, left1), (right0, right1), (value0, value1)
    g, s = lax.axis_index("group"), lax.axis_index("seq")
    me = g * 16 + s
    middle = s < MIDS
    my_chunk = jnp.where(middle, s * 8 + g, 0)
    has_left, has_right = s > 0, s < 15
    early = s < 8

    small = [
        pltpu.make_async_copy(src, dst, in_sem.at[i])
        for i, (src, dst) in enumerate(
            (
                (latent_raw, latent_v),
                (gain, gain_v),
                (lengths, lengths_s),
                (rope_raw, rope_v),
                (trig, trig_v),
                (owner, owner_v),
                (slot, slot_v),
            )
        )
    ]
    for copy in small:
        copy.start()

    def fetches(i):
        return (
            pltpu.make_async_copy(query.at[:, pl.ds(i * QWIDE, QWIDE)], qv.at[i], q_sem.at[i]),
            pltpu.make_async_copy(w_uk.at[:, pl.ds(i * WIDE, WIDE)], kv.at[i], k_sem.at[i]),
            pltpu.make_async_copy(w_uv.at[:, pl.ds(i * WIDE, WIDE)], vv.at[i], v_sem.at[i]),
        )

    def fetched(i):
        for fetch in fetches(i):
            fetch.wait()

    barrier = pltpu.get_barrier_semaphore()

    def greet(device):
        pl.semaphore_signal(barrier, inc=1, device_id=device, device_id_type=MESH)

    @pl.when(middle)
    def _():
        for b in range(16):
            for a in range(8):
                pl.when(me != a * 16 + b)(functools.partial(greet, (a, b)))

    @pl.when(has_left)
    def _():
        greet((g, s - 1))

    for i in range(STEPS):
        for fetch in fetches(i):
            fetch.start()

    row = lax.broadcasted_iota(jnp.int32, (TOK, TOK), 0)
    col = lax.broadcasted_iota(jnp.int32, (TOK, TOK), 1)
    low = col % 64 < 32
    half = col < 64
    odd = row % 2 == 1
    upper = lax.broadcasted_iota(jnp.int32, (8, 128), 0) < 4

    for copy in small[:2]:
        copy.wait()
    source = latent_v[...].astype(F32)
    norm = lax.rsqrt(jnp.mean(source * source, axis=1, keepdims=True) + 1e-06)
    latent = (source * norm * gain_v[...]).astype(BF16)
    lat2[TOK:, :] = latent

    wide = latent.astype(F32)
    plain = [wide[:, i * 128 : (i + 1) * 128] for i in range(4)]
    turned = [pltpu.roll(x, 64, 1) for x in plain]
    moved = [turned[0]] + [jnp.where(half, turned[i - 1], turned[i]) for i in range(1, 4)]

    def chunked(tile):
        for octet in range(8):
            first = ypage[tile, octet * 8 : octet * 8 + 8, :]
            second = ypage[tile, 64 + octet * 8 : 64 + octet * 8 + 8, :]
            xs[tile * QUADS + 2 * octet] = jnp.where(upper, first, pltpu.roll(second, 4, 0)).astype(BF16)
            xs[tile * QUADS + 2 * octet + 1] = jnp.where(upper, pltpu.roll(first, 4, 0), second).astype(BF16)

    for tile, (a, b) in enumerate(zip(plain, moved)):
        ypage[tile] = jnp.where(odd, b, a)
    for tile in range(4):
        chunked(tile)

    pl.semaphore_wait(barrier, 8 * MIDS - jnp.where(middle, 1, 0) + jnp.where(has_right, 1, 0))

    lat_copy = remote(lat2.at[pl.ds(TOK, TOK)], lat2.at[pl.ds(0, TOK)], send_n.at[0], recv_n.at[0], (g, s + 1))
    rope_copy = remote(kr2.at[pl.ds(TOK, TOK)], kr2.at[pl.ds(0, TOK)], send_n.at[1], recv_n.at[1], (g, s + 1))

    def first_hop(b):
        for a in range(8):
            copy = remote(xs.at[b * 8 + a], rs.at[me], send1, recv1, (a, b))
            pl.when(me != a * 16 + b)(copy.start)

    for b in range(8):
        first_hop(b)
        rows, there = pl.ds(TOK + 16 * b, 16), pl.ds(16 * b, 16)
        part = remote(lat2.at[rows], lat2.at[there], send_n.at[0], recv_n.at[0], (g, s + 1))
        pl.when(has_right & early)(part.start)

    for copy in small[2:]:
        copy.wait()
    index = lax.broadcasted_iota(jnp.int32, (8, TOK), 1) + s * TOK
    begin = jnp.zeros((8, TOK), jnp.int32)
    start = jnp.int32(0)
    for r in range(32):
        begin = jnp.where(index >= start, start, begin)
        start = start + lengths_s[0, r]
    pos = (index - begin).astype(F32)
    pos = jnp.concatenate([pos] * 16, axis=0).T.astype(jnp.int32)
    hot = (col == pos).astype(F32).astype(BF16)
    angles = jnp.dot(jnp.concatenate([hot, hot, hot], axis=1), trig_v[...], preferred_element_type=F32)
    cosine, sine = angles[:, :TOK], angles[:, TOK:]
    rope = rope_v[...].astype(F32)
    rope = jnp.concatenate([rope, rope], axis=0).T
    key_rope = rotated(rope, cosine, sine, low).astype(BF16)
    kr2[TOK:, :] = key_rope
    tail = key_rope.astype(F32)
    last_lanes = pltpu.roll(lat2[TOK:, 384:].astype(F32), 64, 1)
    ypage[4] = jnp.where(odd, jnp.where(half, last_lanes, tail), tail)
    chunked(4)
    pl.when(has_right)(rope_copy.start)
    for b in range(8, MIDS):
        first_hop(b)
    pl.when(has_right & jnp.logical_not(early))(lat_copy.start)

    cos_v[...] = cosine
    sin_v[...] = sine
    bias[...] = jnp.where((row - col + TOK) % TOK <= pos, 0.0, -1e30)
    low_m[...] = jnp.where(col <= row, 1.0, 0.0).astype(BF16)
    up_m[...] = jnp.where(col <= row, 0.0, 1.0).astype(BF16)
    for value in valued:
        value[:, :, TOK:] = jnp.ones((HEADS_STEP, 2 * TOK, TOK), BF16)

    @pl.when(middle)
    def _():
        rs[me] = xs[my_chunk]
        want = slot_v[...] * 128 + owner_v[...]
        onehot[...] = (lax.broadcasted_iota(jnp.int32, (512, 256), 0) == want).astype(F32).astype(BF16)

    ahead = s == 4
    def second_hop():
        done(rs.at[pl.ds(0, 127)], recv1)
        rf[...] = rs[...].astype(F32).reshape(1024, 128)
        pages = jnp.concatenate([rf[pl.ds(t, 256, stride=4), :].astype(BF16) for t in range(4)], axis=1)
        picked = jnp.dot(onehot[...], pages, preferred_element_type=F32)
        for t in range(4):
            for k in range(4):
                of[pl.ds(t * 4 + k, 128, stride=16), :] = picked[
                    k * 128 : (k + 1) * 128, t * 128 : (t + 1) * 128
                ]
        os[...] = of[...].reshape(128, 16, 128).astype(BF16)
        cb[my_chunk] = os[me]
        z, x = s // 4, s % 4
        for zh in range(2):
            for xh in range(2):
                for dg in range(8):
                    a = lax.rem(g + dg, 8)
                    for dz in range(2):
                        for dx in range(2):
                            b = (zh * 2 + lax.rem(z + dz, 2)) * 4 + xh * 2 + lax.rem(x + dx, 2)
                            copy = remote(os.at[a * 16 + b], cb.at[my_chunk], send2, recv2, (a, b))
                            if dg + dz + dx:
                                copy.start()
                            else:
                                pl.when((z // 2 != zh) | (x // 2 != xh))(copy.start)

    pl.when(ahead)(second_hop)

    @pl.when(has_left)
    def _():
        done(lat2.at[pl.ds(0, TOK)], recv_n.at[0])
        done(kr2.at[pl.ds(0, TOK)], recv_n.at[1])

    @pl.when(s == 0)
    def _():
        lat2[:TOK, :] = jnp.zeros((TOK, LATENT), BF16)
        kr2[:TOK, :] = jnp.zeros((TOK, TOK), BF16)

    ropes = kr2[...].astype(F32).T
    first_half = lax.broadcasted_iota(jnp.int32, (TOK, 2 * TOK), 0) < 64
    for one in range(2):
        masked = jnp.where(first_half if one == 0 else ~first_half, ropes, 0.0).astype(BF16)
        for right in rights:
            for pair in range(HEADS_STEP // 2):
                right[2 * pair + one, TOK:, :] = masked

    def prepare(i, b, piece):
        pair = piece // 2
        columns = slice(pair * 256, pair * 256 + 256)
        if piece % 2:
            values = jnp.dot(lat2[...], vv[i, :, columns], preferred_element_type=F32).astype(BF16)
            for one in range(2):
                valued[b][2 * pair + one, :, :TOK] = values[:, one * 128 : one * 128 + 128]
            return
        keys = jnp.dot(lat2[...], kv[i, :, columns], preferred_element_type=F32).astype(BF16)
        for one in range(2):
            rights[b][2 * pair + one, :TOK, :] = keys[:, one * 128 : one * 128 + 128].T
        col = lax.broadcasted_iota(jnp.int32, (TOK, TOK), 1)
        half = col < 64
        low = col % 64 < 32
        t0, t1, t2 = [qv[i, :, pl.ds(pair * 384 + t * 128, 128)] for t in range(3)]
        ropes = jnp.where(half, t1, t2).astype(F32)
        turn = rotated(ropes, cos_v[...], sin_v[...], low).astype(BF16)
        second = pltpu.roll(jnp.where(half, t2, t1).astype(F32), 64, 1).astype(BF16)
        for one, nope in enumerate((t0, second)):
            lefts[b][2 * pair + one, :, :TOK] = nope
            lefts[b][2 * pair + one, :, TOK:] = turn

    def scored(b, h):
        row = lax.broadcasted_iota(jnp.int32, (TOK, TOK), 0)
        col = lax.broadcasted_iota(jnp.int32, (TOK, TOK), 1)
        score = jnp.dot(lefts[b][h], rights[b][h], preferred_element_type=F32)
        score_v[h] = jnp.where(col <= row, score[:, TOK:], score[:, :TOK]) + bias[...]

    def softened(h):
        score = score_v[h]
        top = jnp.max(score, axis=1, keepdims=True)
        weight = jnp.exp2((score - top) * SCALE).astype(BF16)
        prob_v[h, :, :TOK] = weight * up_m[...]
        prob_v[h, :, TOK:] = weight * low_m[...]

    def summed(i, b, h):
        got = jnp.dot(prob_v[h], valued[b][h], preferred_element_type=F32)
        out[:, pl.ds(i * WIDE + h * 128, 128)] = (got[:, :TOK] * (1.0 / got[:, TOK:])).astype(BF16)

    def step(i, b, more=True):
        if b == 0:
            fetched(i + 1)
        elif more:
            pl.when(i + 1 < STEPS)(lambda: fetched(i + 1))
        for h in range(HEADS_STEP + 4):
            if h < HEADS_STEP:
                scored(b, h)
            if 0 <= h - 2 < HEADS_STEP:
                softened(h - 2)
            if 0 <= h - 4 < HEADS_STEP:
                summed(i, b, h - 4)
            if more and 0 <= h - 2 < HEADS_STEP:
                prepare(i + 1, 1 - b, h - 2)

    fetched(0)
    for piece in range(HEADS_STEP):
        prepare(0, 0, piece)

    @pl.loop(0, STEPS // 2 - 1)
    def _(j):
        step(2 * j, 0)

        pl.when((j == EVENT // 2) & middle & jnp.logical_not(ahead))(second_hop)

        step(2 * j + 1, 1)

    step(STEPS - 2, 0)
    step(STEPS - 1, 1, more=False)

    @pl.when(middle)
    def _():
        done(cb.at[pl.ds(0, CHUNKS - 1)], recv2)

    @pl.when(jnp.logical_not(middle))
    def _():
        done(cb, recv2)

    chunks[...] = cb[...]

    @pl.when(middle)
    def _():
        done(xs.at[pl.ds(0, CHUNKS - 1)], send1)
        done(os.at[pl.ds(0, 127)], send2)

    @pl.when(jnp.logical_not(middle))
    def _():
        done(xs, send1)

    @pl.when(has_right)
    def _():
        lat_copy.wait_send()
        rope_copy.wait_send()


def written(attended, chunks, attended_out, cache_out, cf, cache_v, sem):
    copies = [
        pltpu.make_async_copy(attended.at[pl.ds(i * 32, 32)], attended_out.at[pl.ds(i * 32, 32)], sem.at[i])
        for i in range(4)
    ]
    for copy in copies:
        copy.start()
    cf[...] = chunks[...].astype(F32).reshape(CHUNKS * 16, 128)
    half4 = lax.broadcasted_iota(jnp.int32, (4, 128), 1) < 64
    for quad in range(QUADS):
        for two in range(2):
            base = (quad * 2 + two) * 9

            def piece(tile, odd):
                return cf[pl.ds((tile * QUADS + quad) * 16 + (2 * two + odd) * 4, 4), :]

            parts = (
                [piece(tile, 0) for tile in range(4)]
                + [jnp.where(half4, piece(4, 0), piece(0, 1))]
                + [piece(tile, 1) for tile in range(1, 5)]
            )
            for k, part in enumerate(parts):
                cache_v[:, (base + k) * 128 : (base + k + 1) * 128] = part.astype(BF16)
    last = pltpu.make_async_copy(cache_v, cache_out, sem.at[4])
    last.start()
    for copy in copies:
        copy.wait()
    last.wait()


def on_device(query, latent_raw, rope_raw, kv_gain, w_uk, w_uv, request_lengths, page_owner, page_slot):
    hbm = pl.BlockSpec(memory_space=pltpu.HBM)
    dma = pltpu.SemaphoreType.DMA

    def b16(*shape):
        return pltpu.VMEM(shape, BF16)

    def f32(*shape):
        return pltpu.VMEM(shape, F32)

    vmem = pl.BlockSpec(memory_space=pltpu.VMEM)
    shapes = (
        jax.ShapeDtypeStruct((TOK, HEADS * 128), BF16),
        jax.ShapeDtypeStruct((4, PAGE_W), BF16),
    )
    attended, chunks = pl.pallas_call(
        kernel,
        out_shape=(pltpu.VMEM(shapes[0].shape, BF16), pltpu.VMEM((CHUNKS, 16, 128), BF16)),
        in_specs=[hbm] * 10,
        out_specs=(vmem, vmem),
        scratch_shapes=[
            pltpu.SMEM((1, 32), jnp.int32),
            f32(1, LATENT),
            b16(TOK, LATENT),
            b16(64, TOK),
            b16(384, 256),
            pltpu.VMEM((1, 256), jnp.int32),
            pltpu.VMEM((1, 256), jnp.int32),
            b16(STEPS, TOK, QWIDE),
            b16(STEPS, LATENT, WIDE),
            b16(STEPS, LATENT, WIDE),
            b16(2 * TOK, LATENT),
            b16(2 * TOK, TOK),
            f32(TOK, TOK),
            f32(TOK, TOK),
            f32(TOK, TOK),
            b16(TOK, TOK),
            b16(TOK, TOK),
            f32(TILES, TOK, 128),
            b16(CHUNKS, 8, 128),
            b16(128, 8, 128),
            f32(1024, 128),
            f32(2048, 128),
            b16(128, 16, 128),
            b16(CHUNKS, 16, 128),
            b16(512, 256),
            b16(HEADS_STEP, TOK, 256),
            b16(HEADS_STEP, TOK, 256),
            b16(HEADS_STEP, 256, 256),
            b16(HEADS_STEP, 256, 256),
            b16(HEADS_STEP, 256, 256),
            b16(HEADS_STEP, 256, 256),
            f32(HEADS_STEP, TOK, TOK),
            b16(HEADS_STEP, TOK, 256),
            dma((7,)),
            dma((STEPS,)),
            dma((STEPS,)),
            dma((STEPS,)),
            dma((2,)),
            dma((2,)),
            dma,
            dma,
            dma,
            dma,
        ],
        compiler_params=pltpu.CompilerParams(
            collective_id=0, has_side_effects=True, vmem_limit_bytes=44 * 2**20
        ),
        name="prefill_and_pages",
    )(
        *(
            pltpu.with_memory_space_constraint(x, pltpu.HBM)
            for x in (
                request_lengths,
                kv_gain.reshape(1, LATENT),
                latent_raw,
                rope_raw.T,
                jnp.asarray(trig_table()),
                page_owner.reshape(1, 256),
                page_slot.reshape(1, 256),
                query,
                w_uk,
                w_uv,
            )
        )
    )
    return pl.pallas_call(
        written,
        out_shape=shapes,
        in_specs=[vmem] * 2,
        out_specs=(hbm, hbm),
        scratch_shapes=[f32(CHUNKS * 16, 128), b16(4, PAGE_W), dma((5,))],
        name="results_out",
    )(
        pltpu.with_memory_space_constraint(attended, pltpu.VMEM), pltpu.with_memory_space_constraint(chunks, pltpu.VMEM)
    )


def solution(mesh):
    rows = P(("group", "seq"), None)
    return jax.shard_map(
        on_device,
        mesh=mesh,
        in_specs=(rows, rows, rows, P(), P(), P(), P("group", None), P(), P()),
        out_specs=(rows, rows),
        check_vma=False,
    )
```

```python
import functools

import jax
import jax.numpy as jnp
import numpy as np
from jax import lax
from jax.experimental import pallas as pl
from jax.experimental.pallas import tpu as pltpu
from jax.sharding import PartitionSpec as P
import ml_dtypes

MESH = pl.DeviceIdType.MESH
F32 = jnp.float32
BF16 = jnp.bfloat16
TOK = 128
HEADS = 64
LATENT = 512
QUADS = 16
TILES = 5
CHUNKS = QUADS * TILES
STEPS = 8
WIDE = 1024
QWIDE = 1536
HEADS_STEP = 8
MIDS = 10
EVENT = 1
PAGE_W = 36864
SCALE = float(1.0 / 192.0**0.5 * np.log2(np.e))


def trig_table():
    freqs = (10000.0 ** (-np.arange(32, dtype=np.float64) / 32.0)).astype(np.float32)
    angle = np.arange(TOK, dtype=np.float32)[:, None] * freqs[None, :]
    cosine = np.cos(angle.astype(np.float64)).astype(np.float32)
    sine = np.sin(angle.astype(np.float64)).astype(np.float32)
    full = np.concatenate([cosine] * 4 + [-sine, sine, -sine, sine], axis=1)
    parts = []
    for _ in range(3):
        part = full.astype(ml_dtypes.bfloat16)
        parts.append(part)
        full = full - part.astype(np.float32)
    return np.concatenate(parts, axis=0)


def remote(src, dst, send, recv, device):
    return pltpu.make_async_remote_copy(
        src_ref=src, dst_ref=dst, send_sem=send, recv_sem=recv, device_id=device, device_id_type=MESH
    )


def done(ref, sem):
    pltpu.make_async_copy(ref, ref, sem).wait()


def rotated(x, cosine, sine, low):
    partner = jnp.where(low, pltpu.roll(x, 96, 1), pltpu.roll(x, 32, 1))
    return x * cosine + partner * sine


def kernel(
    lengths, gain, latent_raw, rope_raw, trig, owner, slot, query, w_uk, w_uv,
    out, chunks,
    lengths_s, gain_v, latent_v, rope_v, trig_v, owner_v, slot_v,
    qv, kv, vv, lat2, kr2, cos_v, sin_v, bias, low_m, up_m, ypage, xs, rs, rf, of, os, cb, onehot,
    left0, left1, right0, right1, value0, value1, score_v, prob_v,
    in_sem, q_sem, k_sem, v_sem, send_n, recv_n, send1, recv1, send2, recv2,
):
    lefts, rights, valued = (left0, left1), (right0, right1), (value0, value1)
    g, s = lax.axis_index("group"), lax.axis_index("seq")
    me = g * 16 + s
    middle = s < MIDS
    my_chunk = jnp.where(middle, s * 8 + g, 0)
    has_left, has_right = s > 0, s < 15
    early = s < 8

    small = [
        pltpu.make_async_copy(src, dst, in_sem.at[i])
        for i, (src, dst) in enumerate(
            (
                (latent_raw, latent_v),
                (gain, gain_v),
                (lengths, lengths_s),
                (rope_raw, rope_v),
                (trig, trig_v),
                (owner, owner_v),
                (slot, slot_v),
            )
        )
    ]
    for copy in small:
        copy.start()

    def fetches(i):
        return (
            pltpu.make_async_copy(query.at[:, pl.ds(i * QWIDE, QWIDE)], qv.at[i], q_sem.at[i]),
            pltpu.make_async_copy(w_uk.at[:, pl.ds(i * WIDE, WIDE)], kv.at[i], k_sem.at[i]),
            pltpu.make_async_copy(w_uv.at[:, pl.ds(i * WIDE, WIDE)], vv.at[i], v_sem.at[i]),
        )

    def fetched(i):
        for fetch in fetches(i):
            fetch.wait()

    barrier = pltpu.get_barrier_semaphore()

    def greet(device):
        pl.semaphore_signal(barrier, inc=1, device_id=device, device_id_type=MESH)

    @pl.when(middle)
    def _():
        for b in range(16):
            for a in range(8):
                pl.when(me != a * 16 + b)(functools.partial(greet, (a, b)))

    @pl.when(has_left)
    def _():
        greet((g, s - 1))

    for i in range(STEPS):
        for fetch in fetches(i):
            fetch.start()

    row = lax.broadcasted_iota(jnp.int32, (TOK, TOK), 0)
    col = lax.broadcasted_iota(jnp.int32, (TOK, TOK), 1)
    low = col % 64 < 32
    half = col < 64
    odd = row % 2 == 1
    upper = lax.broadcasted_iota(jnp.int32, (8, 128), 0) < 4

    for copy in small[:2]:
        copy.wait()
    source = latent_v[...].astype(F32)
    norm = lax.rsqrt(jnp.mean(source * source, axis=1, keepdims=True) + 1e-06)
    latent = (source * norm * gain_v[...]).astype(BF16)
    lat2[TOK:, :] = latent

    wide = latent.astype(F32)
    plain = [wide[:, i * 128 : (i + 1) * 128] for i in range(4)]
    turned = [pltpu.roll(x, 64, 1) for x in plain]
    moved = [turned[0]] + [jnp.where(half, turned[i - 1], turned[i]) for i in range(1, 4)]

    def chunked(tile):
        for octet in range(8):
            first = ypage[tile, octet * 8 : octet * 8 + 8, :]
            second = ypage[tile, 64 + octet * 8 : 64 + octet * 8 + 8, :]
            xs[tile * QUADS + 2 * octet] = jnp.where(upper, first, pltpu.roll(second, 4, 0)).astype(BF16)
            xs[tile * QUADS + 2 * octet + 1] = jnp.where(upper, pltpu.roll(first, 4, 0), second).astype(BF16)

    for tile, (a, b) in enumerate(zip(plain, moved)):
        ypage[tile] = jnp.where(odd, b, a)
    for tile in range(4):
        chunked(tile)

    pl.semaphore_wait(barrier, 8 * MIDS - jnp.where(middle, 1, 0) + jnp.where(has_right, 1, 0))

    lat_copy = remote(lat2.at[pl.ds(TOK, TOK)], lat2.at[pl.ds(0, TOK)], send_n.at[0], recv_n.at[0], (g, s + 1))
    rope_copy = remote(kr2.at[pl.ds(TOK, TOK)], kr2.at[pl.ds(0, TOK)], send_n.at[1], recv_n.at[1], (g, s + 1))

    def first_hop(b):
        for a in range(8):
            copy = remote(xs.at[b * 8 + a], rs.at[me], send1, recv1, (a, b))
            pl.when(me != a * 16 + b)(copy.start)

    for b in range(8):
        first_hop(b)
        rows, there = pl.ds(TOK + 16 * b, 16), pl.ds(16 * b, 16)
        part = remote(lat2.at[rows], lat2.at[there], send_n.at[0], recv_n.at[0], (g, s + 1))
        pl.when(has_right & early)(part.start)

    for copy in small[2:]:
        copy.wait()
    index = lax.broadcasted_iota(jnp.int32, (8, TOK), 1) + s * TOK
    begin = jnp.zeros((8, TOK), jnp.int32)
    start = jnp.int32(0)
    for r in range(32):
        begin = jnp.where(index >= start, start, begin)
        start = start + lengths_s[0, r]
    pos = (index - begin).astype(F32)
    pos = jnp.concatenate([pos] * 16, axis=0).T.astype(jnp.int32)
    hot = (col == pos).astype(F32).astype(BF16)
    angles = jnp.dot(jnp.concatenate([hot, hot, hot], axis=1), trig_v[...], preferred_element_type=F32)
    cosine, sine = angles[:, :TOK], angles[:, TOK:]
    rope = rope_v[...].astype(F32)
    rope = jnp.concatenate([rope, rope], axis=0).T
    key_rope = rotated(rope, cosine, sine, low).astype(BF16)
    kr2[TOK:, :] = key_rope
    tail = key_rope.astype(F32)
    last_lanes = pltpu.roll(lat2[TOK:, 384:].astype(F32), 64, 1)
    ypage[4] = jnp.where(odd, jnp.where(half, last_lanes, tail), tail)
    chunked(4)
    pl.when(has_right)(rope_copy.start)
    for b in range(8, MIDS):
        first_hop(b)
    pl.when(has_right & jnp.logical_not(early))(lat_copy.start)

    cos_v[...] = cosine
    sin_v[...] = sine
    bias[...] = jnp.where((row - col + TOK) % TOK <= pos, 0.0, -1e30)
    low_m[...] = jnp.where(col <= row, 1.0, 0.0).astype(BF16)
    up_m[...] = jnp.where(col <= row, 0.0, 1.0).astype(BF16)
    for value in valued:
        value[:, :, TOK:] = jnp.ones((HEADS_STEP, 2 * TOK, TOK), BF16)

    @pl.when(middle)
    def _():
        rs[me] = xs[my_chunk]
        want = slot_v[...] * 128 + owner_v[...]
        onehot[...] = (lax.broadcasted_iota(jnp.int32, (512, 256), 0) == want).astype(F32).astype(BF16)

    ahead = s == 4
    def second_hop():
        done(rs.at[pl.ds(0, 127)], recv1)
        rf[...] = rs[...].astype(F32).reshape(1024, 128)
        pages = jnp.concatenate([rf[pl.ds(t, 256, stride=4), :].astype(BF16) for t in range(4)], axis=1)
        picked = jnp.dot(onehot[...], pages, preferred_element_type=F32)
        for t in range(4):
            for k in range(4):
                of[pl.ds(t * 4 + k, 128, stride=16), :] = picked[
                    k * 128 : (k + 1) * 128, t * 128 : (t + 1) * 128
                ]
        os[...] = of[...].reshape(128, 16, 128).astype(BF16)
        cb[my_chunk] = os[me]
        z, x = s // 4, s % 4
        y = g // 2

        def go(a, c, other):
            copy = remote(os.at[a * 16 + c], cb.at[my_chunk], send2, recv2, (a, c))
            if other is None:
                copy.start()
            else:
                pl.when(other)(copy.start)

        for zh in range(2):
            for yh in range(2):
                for dz in range(2):
                    for dg in range(4):
                        for dx in range(4):
                            a = yh * 4 + lax.rem(g + dg, 4)
                            c = (zh * 2 + lax.rem(z + dz, 2)) * 4 + lax.rem(x + dx, 4)
                            go(a, c, None if dg + dz + dx else (z // 2 != zh) | (g // 4 != yh))

    pl.when(ahead)(second_hop)

    @pl.when(has_left)
    def _():
        done(lat2.at[pl.ds(0, TOK)], recv_n.at[0])
        done(kr2.at[pl.ds(0, TOK)], recv_n.at[1])

    @pl.when(s == 0)
    def _():
        lat2[:TOK, :] = jnp.zeros((TOK, LATENT), BF16)
        kr2[:TOK, :] = jnp.zeros((TOK, TOK), BF16)

    ropes = kr2[...].astype(F32).T
    first_half = lax.broadcasted_iota(jnp.int32, (TOK, 2 * TOK), 0) < 64
    for one in range(2):
        masked = jnp.where(first_half if one == 0 else ~first_half, ropes, 0.0).astype(BF16)
        for right in rights:
            for pair in range(HEADS_STEP // 2):
                right[2 * pair + one, TOK:, :] = masked

    def prepare(i, b, piece):
        pair = piece // 2
        columns = slice(pair * 256, pair * 256 + 256)
        if piece % 2:
            values = jnp.dot(lat2[...], vv[i, :, columns], preferred_element_type=F32).astype(BF16)
            for one in range(2):
                valued[b][2 * pair + one, :, :TOK] = values[:, one * 128 : one * 128 + 128]
            return
        keys = jnp.dot(lat2[...], kv[i, :, columns], preferred_element_type=F32).astype(BF16)
        for one in range(2):
            rights[b][2 * pair + one, :TOK, :] = keys[:, one * 128 : one * 128 + 128].T
        col = lax.broadcasted_iota(jnp.int32, (TOK, TOK), 1)
        half = col < 64
        low = col % 64 < 32
        t0, t1, t2 = [qv[i, :, pl.ds(pair * 384 + t * 128, 128)] for t in range(3)]
        ropes = jnp.where(half, t1, t2).astype(F32)
        turn = rotated(ropes, cos_v[...], sin_v[...], low).astype(BF16)
        second = pltpu.roll(jnp.where(half, t2, t1).astype(F32), 64, 1).astype(BF16)
        for one, nope in enumerate((t0, second)):
            lefts[b][2 * pair + one, :, :TOK] = nope
            lefts[b][2 * pair + one, :, TOK:] = turn

    def scored(b, h):
        row = lax.broadcasted_iota(jnp.int32, (TOK, TOK), 0)
        col = lax.broadcasted_iota(jnp.int32, (TOK, TOK), 1)
        score = jnp.dot(lefts[b][h], rights[b][h], preferred_element_type=F32)
        score_v[h] = jnp.where(col <= row, score[:, TOK:], score[:, :TOK]) + bias[...]

    def softened(h):
        score = score_v[h]
        top = jnp.max(score, axis=1, keepdims=True)
        weight = jnp.exp2((score - top) * SCALE).astype(BF16)
        prob_v[h, :, :TOK] = weight * up_m[...]
        prob_v[h, :, TOK:] = weight * low_m[...]

    def summed(i, b, h):
        got = jnp.dot(prob_v[h], valued[b][h], preferred_element_type=F32)
        out[:, pl.ds(i * WIDE + h * 128, 128)] = (got[:, :TOK] * (1.0 / got[:, TOK:])).astype(BF16)

    def step(i, b, more=True):
        if b == 0:
            fetched(i + 1)
        elif more:
            pl.when(i + 1 < STEPS)(lambda: fetched(i + 1))
        for h in range(HEADS_STEP + 4):
            if h < HEADS_STEP:
                scored(b, h)
            if 0 <= h - 2 < HEADS_STEP:
                softened(h - 2)
            if 0 <= h - 4 < HEADS_STEP:
                summed(i, b, h - 4)
            if more and 0 <= h - 2 < HEADS_STEP:
                prepare(i + 1, 1 - b, h - 2)

    fetched(0)
    for piece in range(HEADS_STEP):
        prepare(0, 0, piece)

    @pl.loop(0, STEPS // 2 - 1)
    def _(j):
        step(2 * j, 0)

        pl.when((j == EVENT // 2) & middle & jnp.logical_not(ahead))(second_hop)

        step(2 * j + 1, 1)

    step(STEPS - 2, 0)
    step(STEPS - 1, 1, more=False)

    @pl.when(middle)
    def _():
        done(cb.at[pl.ds(0, CHUNKS - 1)], recv2)

    @pl.when(jnp.logical_not(middle))
    def _():
        done(cb, recv2)

    chunks[...] = cb[...]

    @pl.when(middle)
    def _():
        done(xs.at[pl.ds(0, CHUNKS - 1)], send1)
        done(os.at[pl.ds(0, 127)], send2)

    @pl.when(jnp.logical_not(middle))
    def _():
        done(xs, send1)

    @pl.when(has_right)
    def _():
        lat_copy.wait_send()
        rope_copy.wait_send()


def written(attended, chunks, attended_out, cache_out, cf, cache_v, sem):
    copies = [
        pltpu.make_async_copy(attended.at[pl.ds(i * 32, 32)], attended_out.at[pl.ds(i * 32, 32)], sem.at[i])
        for i in range(4)
    ]
    for copy in copies:
        copy.start()
    cf[...] = chunks[...].astype(F32).reshape(CHUNKS * 16, 128)
    half4 = lax.broadcasted_iota(jnp.int32, (4, 128), 1) < 64
    for quad in range(QUADS):
        for two in range(2):
            base = (quad * 2 + two) * 9

            def piece(tile, odd):
                return cf[pl.ds((tile * QUADS + quad) * 16 + (2 * two + odd) * 4, 4), :]

            parts = (
                [piece(tile, 0) for tile in range(4)]
                + [jnp.where(half4, piece(4, 0), piece(0, 1))]
                + [piece(tile, 1) for tile in range(1, 5)]
            )
            for k, part in enumerate(parts):
                cache_v[:, (base + k) * 128 : (base + k + 1) * 128] = part.astype(BF16)
    last = pltpu.make_async_copy(cache_v, cache_out, sem.at[4])
    last.start()
    for copy in copies:
        copy.wait()
    last.wait()


def on_device(query, latent_raw, rope_raw, kv_gain, w_uk, w_uv, request_lengths, page_owner, page_slot):
    hbm = pl.BlockSpec(memory_space=pltpu.HBM)
    dma = pltpu.SemaphoreType.DMA

    def b16(*shape):
        return pltpu.VMEM(shape, BF16)

    def f32(*shape):
        return pltpu.VMEM(shape, F32)

    vmem = pl.BlockSpec(memory_space=pltpu.VMEM)
    shapes = (
        jax.ShapeDtypeStruct((TOK, HEADS * 128), BF16),
        jax.ShapeDtypeStruct((4, PAGE_W), BF16),
    )
    attended, chunks = pl.pallas_call(
        kernel,
        out_shape=(pltpu.VMEM(shapes[0].shape, BF16), pltpu.VMEM((CHUNKS, 16, 128), BF16)),
        in_specs=[hbm] * 10,
        out_specs=(vmem, vmem),
        scratch_shapes=[
            pltpu.SMEM((1, 32), jnp.int32),
            f32(1, LATENT),
            b16(TOK, LATENT),
            b16(64, TOK),
            b16(384, 256),
            pltpu.VMEM((1, 256), jnp.int32),
            pltpu.VMEM((1, 256), jnp.int32),
            b16(STEPS, TOK, QWIDE),
            b16(STEPS, LATENT, WIDE),
            b16(STEPS, LATENT, WIDE),
            b16(2 * TOK, LATENT),
            b16(2 * TOK, TOK),
            f32(TOK, TOK),
            f32(TOK, TOK),
            f32(TOK, TOK),
            b16(TOK, TOK),
            b16(TOK, TOK),
            f32(TILES, TOK, 128),
            b16(CHUNKS, 8, 128),
            b16(128, 8, 128),
            f32(1024, 128),
            f32(2048, 128),
            b16(128, 16, 128),
            b16(CHUNKS, 16, 128),
            b16(512, 256),
            b16(HEADS_STEP, TOK, 256),
            b16(HEADS_STEP, TOK, 256),
            b16(HEADS_STEP, 256, 256),
            b16(HEADS_STEP, 256, 256),
            b16(HEADS_STEP, 256, 256),
            b16(HEADS_STEP, 256, 256),
            f32(HEADS_STEP, TOK, TOK),
            b16(HEADS_STEP, TOK, 256),
            dma((7,)),
            dma((STEPS,)),
            dma((STEPS,)),
            dma((STEPS,)),
            dma((2,)),
            dma((2,)),
            dma,
            dma,
            dma,
            dma,
        ],
        compiler_params=pltpu.CompilerParams(
            collective_id=0, has_side_effects=True, vmem_limit_bytes=44 * 2**20
        ),
        name="prefill_and_pages",
    )(
        *(
            pltpu.with_memory_space_constraint(x, pltpu.HBM)
            for x in (
                request_lengths,
                kv_gain.reshape(1, LATENT),
                latent_raw,
                rope_raw.T,
                jnp.asarray(trig_table()),
                page_owner.reshape(1, 256),
                page_slot.reshape(1, 256),
                query,
                w_uk,
                w_uv,
            )
        )
    )
    return pl.pallas_call(
        written,
        out_shape=shapes,
        in_specs=[vmem] * 2,
        out_specs=(hbm, hbm),
        scratch_shapes=[f32(CHUNKS * 16, 128), b16(4, PAGE_W), dma((5,))],
        name="results_out",
    )(
        pltpu.with_memory_space_constraint(attended, pltpu.VMEM), pltpu.with_memory_space_constraint(chunks, pltpu.VMEM)
    )


def solution(mesh):
    rows = P(("group", "seq"), None)
    return jax.shard_map(
        on_device,
        mesh=mesh,
        in_specs=(rows, rows, rows, P(), P(), P(), P("group", None), P(), P()),
        out_specs=(rows, rows),
        check_vma=False,
    )
```

```python
import functools

import jax
import jax.numpy as jnp
import numpy as np
from jax import lax
from jax.experimental import pallas as pl
from jax.experimental.pallas import tpu as pltpu
from jax.sharding import PartitionSpec as P
import ml_dtypes

MESH = pl.DeviceIdType.MESH
F32 = jnp.float32
BF16 = jnp.bfloat16
TOK = 128
HEADS = 64
LATENT = 512
QUADS = 16
TILES = 5
CHUNKS = QUADS * TILES
STEPS = 8
WIDE = 1024
QWIDE = 1536
HEADS_STEP = 8
MIDS = 10
EVENT = 1
PAGE_W = 36864
SCALE = float(1.0 / 192.0**0.5 * np.log2(np.e))


def trig_table():
    freqs = (10000.0 ** (-np.arange(32, dtype=np.float64) / 32.0)).astype(np.float32)
    angle = np.arange(TOK, dtype=np.float32)[:, None] * freqs[None, :]
    cosine = np.cos(angle.astype(np.float64)).astype(np.float32)
    sine = np.sin(angle.astype(np.float64)).astype(np.float32)
    full = np.concatenate([cosine] * 4 + [-sine, sine, -sine, sine], axis=1)
    parts = []
    for _ in range(3):
        part = full.astype(ml_dtypes.bfloat16)
        parts.append(part)
        full = full - part.astype(np.float32)
    return np.concatenate(parts, axis=0)


def remote(src, dst, send, recv, device):
    return pltpu.make_async_remote_copy(
        src_ref=src, dst_ref=dst, send_sem=send, recv_sem=recv, device_id=device, device_id_type=MESH
    )


def done(ref, sem):
    pltpu.make_async_copy(ref, ref, sem).wait()


def rotated(x, cosine, sine, low):
    partner = jnp.where(low, pltpu.roll(x, 96, 1), pltpu.roll(x, 32, 1))
    return x * cosine + partner * sine


def kernel(
    lengths, gain, latent_raw, rope_raw, trig, owner, slot, query, w_uk, w_uv,
    out, chunks,
    lengths_s, gain_v, latent_v, rope_v, trig_v, owner_v, slot_v,
    qv, kv, vv, lat2, kr2, krp, cos_v, sin_v, bias, low_m, up_m, ypage, xs, rs, rf, of, os, cb, onehot,
    left0, left1, right0, right1, value0, value1, score_v, prob_v,
    in_sem, q_sem, k_sem, v_sem, send_n, recv_n, send1, recv1, send2, recv2,
):
    lefts, rights, valued = (left0, left1), (right0, right1), (value0, value1)
    g, s = lax.axis_index("group"), lax.axis_index("seq")
    me = g * 16 + s
    middle = s < MIDS
    my_chunk = jnp.where(middle, s * 8 + g, 0)
    has_left, has_right = s > 0, s < 15
    early = s < 8

    small = [
        pltpu.make_async_copy(src, dst, in_sem.at[i])
        for i, (src, dst) in enumerate(
            (
                (latent_raw, latent_v),
                (gain, gain_v),
                (lengths, lengths_s),
                (rope_raw, rope_v),
                (trig, trig_v),
                (owner, owner_v),
                (slot, slot_v),
            )
        )
    ]
    for copy in small:
        copy.start()

    def fetches(i):
        return (
            pltpu.make_async_copy(query.at[:, pl.ds(i * QWIDE, QWIDE)], qv.at[i], q_sem.at[i]),
            pltpu.make_async_copy(w_uk.at[:, pl.ds(i * WIDE, WIDE)], kv.at[i], k_sem.at[i]),
            pltpu.make_async_copy(w_uv.at[:, pl.ds(i * WIDE, WIDE)], vv.at[i], v_sem.at[i]),
        )

    def fetched(i):
        for fetch in fetches(i):
            fetch.wait()

    barrier = pltpu.get_barrier_semaphore()

    def greet(device):
        pl.semaphore_signal(barrier, inc=1, device_id=device, device_id_type=MESH)

    @pl.when(middle)
    def _():
        for b in range(16):
            for a in range(8):
                pl.when(me != a * 16 + b)(functools.partial(greet, (a, b)))

    @pl.when(has_left)
    def _():
        greet((g, s - 1))

    for i in range(STEPS):
        for fetch in fetches(i):
            fetch.start()

    row = lax.broadcasted_iota(jnp.int32, (TOK, TOK), 0)
    col = lax.broadcasted_iota(jnp.int32, (TOK, TOK), 1)
    low = col % 64 < 32
    half = col < 64
    odd = row % 2 == 1
    upper = lax.broadcasted_iota(jnp.int32, (8, 128), 0) < 4

    for copy in small[:2]:
        copy.wait()
    source = latent_v[...].astype(F32)
    norm = lax.rsqrt(jnp.mean(source * source, axis=1, keepdims=True) + 1e-06)
    latent = (source * norm * gain_v[...]).astype(BF16)
    lat2[TOK:, :] = latent

    wide = latent.astype(F32)
    plain = [wide[:, i * 128 : (i + 1) * 128] for i in range(4)]
    turned = [pltpu.roll(x, 64, 1) for x in plain]
    moved = [turned[0]] + [jnp.where(half, turned[i - 1], turned[i]) for i in range(1, 4)]

    def chunked(tile):
        for octet in range(8):
            first = ypage[tile, octet * 8 : octet * 8 + 8, :]
            second = ypage[tile, 64 + octet * 8 : 64 + octet * 8 + 8, :]
            xs[tile * QUADS + 2 * octet] = jnp.where(upper, first, pltpu.roll(second, 4, 0)).astype(BF16)
            xs[tile * QUADS + 2 * octet + 1] = jnp.where(upper, pltpu.roll(first, 4, 0), second).astype(BF16)

    for tile, (a, b) in enumerate(zip(plain, moved)):
        ypage[tile] = jnp.where(odd, b, a)
    for tile in range(4):
        chunked(tile)

    pl.semaphore_wait(barrier, 8 * MIDS - jnp.where(middle, 1, 0) + jnp.where(has_right, 1, 0))

    lat_copy = remote(lat2.at[pl.ds(TOK, TOK)], lat2.at[pl.ds(0, TOK)], send_n.at[0], recv_n.at[0], (g, s + 1))
    rope_copy = remote(krp.at[pl.ds(64, 64)], krp.at[pl.ds(0, 64)], send_n.at[1], recv_n.at[1], (g, s + 1))

    def first_hop(b):
        for a in range(8):
            copy = remote(xs.at[b * 8 + a], rs.at[me], send1, recv1, (a, b))
            pl.when(me != a * 16 + b)(copy.start)

    for b in range(8):
        first_hop(b)
        rows, there = pl.ds(TOK + 16 * b, 16), pl.ds(16 * b, 16)
        part = remote(lat2.at[rows], lat2.at[there], send_n.at[0], recv_n.at[0], (g, s + 1))
        pl.when(has_right & early)(part.start)

    for copy in small[2:]:
        copy.wait()
    index = lax.broadcasted_iota(jnp.int32, (8, TOK), 1) + s * TOK
    begin = jnp.zeros((8, TOK), jnp.int32)
    start = jnp.int32(0)
    for r in range(32):
        begin = jnp.where(index >= start, start, begin)
        start = start + lengths_s[0, r]
    pos = (index - begin).astype(F32)
    pos = jnp.concatenate([pos] * 16, axis=0).T.astype(jnp.int32)
    hot = (col == pos).astype(F32).astype(BF16)
    angles = jnp.dot(jnp.concatenate([hot, hot, hot], axis=1), trig_v[...], preferred_element_type=F32)
    cosine, sine = angles[:, :TOK], angles[:, TOK:]
    rope = rope_v[...].astype(F32)
    rope = jnp.concatenate([rope, rope], axis=0).T
    key_rope = rotated(rope, cosine, sine, low).astype(BF16)
    kr2[TOK:, :] = key_rope
    tail = key_rope.astype(F32)
    krp[64:, :] = jnp.where(half[:64], tail[:64], tail[64:]).astype(BF16)
    last_lanes = pltpu.roll(lat2[TOK:, 384:].astype(F32), 64, 1)
    ypage[4] = jnp.where(odd, jnp.where(half, last_lanes, tail), tail)
    chunked(4)
    pl.when(has_right)(rope_copy.start)
    for b in range(8, MIDS):
        first_hop(b)
    pl.when(has_right & jnp.logical_not(early))(lat_copy.start)

    cos_v[...] = cosine
    sin_v[...] = sine
    bias[...] = jnp.where((row - col + TOK) % TOK <= pos, 0.0, -1e30)
    low_m[...] = jnp.where(col <= row, 1.0, 0.0).astype(BF16)
    up_m[...] = jnp.where(col <= row, 0.0, 1.0).astype(BF16)
    for value in valued:
        value[:, :, TOK:] = jnp.ones((HEADS_STEP, 2 * TOK, TOK), BF16)

    @pl.when(middle)
    def _():
        rs[me] = xs[my_chunk]
        want = slot_v[...] * 128 + owner_v[...]
        onehot[...] = (lax.broadcasted_iota(jnp.int32, (512, 256), 0) == want).astype(F32).astype(BF16)

    ahead = s == 4
    def second_hop():
        done(rs.at[pl.ds(0, 127)], recv1)
        rf[...] = rs[...].astype(F32).reshape(1024, 128)
        pages = jnp.concatenate([rf[pl.ds(t, 256, stride=4), :].astype(BF16) for t in range(4)], axis=1)
        picked = jnp.dot(onehot[...], pages, preferred_element_type=F32)
        for t in range(4):
            for k in range(4):
                of[pl.ds(t * 4 + k, 128, stride=16), :] = picked[
                    k * 128 : (k + 1) * 128, t * 128 : (t + 1) * 128
                ]
        os[...] = of[...].reshape(128, 16, 128).astype(BF16)
        cb[my_chunk] = os[me]
        z, x = s // 4, s % 4
        y = g // 2

        def go(a, c, other):
            copy = remote(os.at[a * 16 + c], cb.at[my_chunk], send2, recv2, (a, c))
            if other is None:
                copy.start()
            else:
                pl.when(other)(copy.start)

        for zh in range(2):
            for yh in range(2):
                for dz in range(2):
                    for dg in range(4):
                        for dx in range(4):
                            a = yh * 4 + lax.rem(g + dg, 4)
                            c = (zh * 2 + lax.rem(z + dz, 2)) * 4 + lax.rem(x + dx, 4)
                            go(a, c, None if dg + dz + dx else (z // 2 != zh) | (g // 4 != yh))

    pl.when(ahead)(second_hop)

    @pl.when(has_left)
    def _():
        done(lat2.at[pl.ds(0, TOK)], recv_n.at[0])
        done(krp.at[pl.ds(0, 64)], recv_n.at[1])
        packed = krp[:64, :].astype(F32)
        swapped = pltpu.roll(packed, 64, 1)
        kr2[:64, :] = jnp.where(half[:64], packed, swapped).astype(BF16)
        kr2[64:TOK, :] = jnp.where(half[:64], swapped, packed).astype(BF16)

    @pl.when(s == 0)
    def _():
        lat2[:TOK, :] = jnp.zeros((TOK, LATENT), BF16)
        kr2[:TOK, :] = jnp.zeros((TOK, TOK), BF16)

    ropes = kr2[...].astype(F32).T
    first_half = lax.broadcasted_iota(jnp.int32, (TOK, 2 * TOK), 0) < 64
    for one in range(2):
        masked = jnp.where(first_half if one == 0 else ~first_half, ropes, 0.0).astype(BF16)
        for right in rights:
            for pair in range(HEADS_STEP // 2):
                right[2 * pair + one, TOK:, :] = masked

    def prepare(i, b, piece):
        pair = piece // 2
        columns = slice(pair * 256, pair * 256 + 256)
        if piece % 2:
            values = jnp.dot(lat2[...], vv[i, :, columns], preferred_element_type=F32).astype(BF16)
            for one in range(2):
                valued[b][2 * pair + one, :, :TOK] = values[:, one * 128 : one * 128 + 128]
            return
        keys = jnp.dot(lat2[...], kv[i, :, columns], preferred_element_type=F32).astype(BF16)
        for one in range(2):
            rights[b][2 * pair + one, :TOK, :] = keys[:, one * 128 : one * 128 + 128].T
        col = lax.broadcasted_iota(jnp.int32, (TOK, TOK), 1)
        half = col < 64
        low = col % 64 < 32
        t0, t1, t2 = [qv[i, :, pl.ds(pair * 384 + t * 128, 128)] for t in range(3)]
        ropes = jnp.where(half, t1, t2).astype(F32)
        turn = rotated(ropes, cos_v[...], sin_v[...], low).astype(BF16)
        second = pltpu.roll(jnp.where(half, t2, t1).astype(F32), 64, 1).astype(BF16)
        for one, nope in enumerate((t0, second)):
            lefts[b][2 * pair + one, :, :TOK] = nope
            lefts[b][2 * pair + one, :, TOK:] = turn

    def scored(b, h):
        row = lax.broadcasted_iota(jnp.int32, (TOK, TOK), 0)
        col = lax.broadcasted_iota(jnp.int32, (TOK, TOK), 1)
        score = jnp.dot(lefts[b][h], rights[b][h], preferred_element_type=F32)
        score_v[h] = jnp.where(col <= row, score[:, TOK:], score[:, :TOK]) + bias[...]

    def softened(h):
        score = score_v[h]
        top = jnp.max(score, axis=1, keepdims=True)
        weight = jnp.exp2((score - top) * SCALE).astype(BF16)
        prob_v[h, :, :TOK] = weight * up_m[...]
        prob_v[h, :, TOK:] = weight * low_m[...]

    def summed(i, b, h):
        got = jnp.dot(prob_v[h], valued[b][h], preferred_element_type=F32)
        out[:, pl.ds(i * WIDE + h * 128, 128)] = (got[:, :TOK] * (1.0 / got[:, TOK:])).astype(BF16)

    def step(i, b, more=True):
        if b == 0:
            fetched(i + 1)
        elif more:
            pl.when(i + 1 < STEPS)(lambda: fetched(i + 1))
        for h in range(HEADS_STEP + 4):
            if h < HEADS_STEP:
                scored(b, h)
            if 0 <= h - 2 < HEADS_STEP:
                softened(h - 2)
            if 0 <= h - 4 < HEADS_STEP:
                summed(i, b, h - 4)
            if more and 0 <= h - 2 < HEADS_STEP:
                prepare(i + 1, 1 - b, h - 2)

    fetched(0)
    for piece in range(HEADS_STEP):
        prepare(0, 0, piece)

    @pl.loop(0, STEPS // 2 - 1)
    def _(j):
        step(2 * j, 0)

        pl.when((j == EVENT // 2) & middle & jnp.logical_not(ahead))(second_hop)

        step(2 * j + 1, 1)

    step(STEPS - 2, 0)
    step(STEPS - 1, 1, more=False)

    @pl.when(middle)
    def _():
        done(cb.at[pl.ds(0, CHUNKS - 1)], recv2)

    @pl.when(jnp.logical_not(middle))
    def _():
        done(cb, recv2)

    chunks[...] = cb[...]

    @pl.when(middle)
    def _():
        done(xs.at[pl.ds(0, CHUNKS - 1)], send1)
        done(os.at[pl.ds(0, 127)], send2)

    @pl.when(jnp.logical_not(middle))
    def _():
        done(xs, send1)

    @pl.when(has_right)
    def _():
        lat_copy.wait_send()
        rope_copy.wait_send()


def written(attended, chunks, attended_out, cache_out, cf, cache_v, sem):
    copies = [
        pltpu.make_async_copy(attended.at[pl.ds(i * 32, 32)], attended_out.at[pl.ds(i * 32, 32)], sem.at[i])
        for i in range(4)
    ]
    for copy in copies:
        copy.start()
    cf[...] = chunks[...].astype(F32).reshape(CHUNKS * 16, 128)
    half4 = lax.broadcasted_iota(jnp.int32, (4, 128), 1) < 64
    for quad in range(QUADS):
        for two in range(2):
            base = (quad * 2 + two) * 9

            def piece(tile, odd):
                return cf[pl.ds((tile * QUADS + quad) * 16 + (2 * two + odd) * 4, 4), :]

            parts = (
                [piece(tile, 0) for tile in range(4)]
                + [jnp.where(half4, piece(4, 0), piece(0, 1))]
                + [piece(tile, 1) for tile in range(1, 5)]
            )
            for k, part in enumerate(parts):
                cache_v[:, (base + k) * 128 : (base + k + 1) * 128] = part.astype(BF16)
    last = pltpu.make_async_copy(cache_v, cache_out, sem.at[4])
    last.start()
    for copy in copies:
        copy.wait()
    last.wait()


def on_device(query, latent_raw, rope_raw, kv_gain, w_uk, w_uv, request_lengths, page_owner, page_slot):
    hbm = pl.BlockSpec(memory_space=pltpu.HBM)
    dma = pltpu.SemaphoreType.DMA

    def b16(*shape):
        return pltpu.VMEM(shape, BF16)

    def f32(*shape):
        return pltpu.VMEM(shape, F32)

    vmem = pl.BlockSpec(memory_space=pltpu.VMEM)
    shapes = (
        jax.ShapeDtypeStruct((TOK, HEADS * 128), BF16),
        jax.ShapeDtypeStruct((4, PAGE_W), BF16),
    )
    attended, chunks = pl.pallas_call(
        kernel,
        out_shape=(pltpu.VMEM(shapes[0].shape, BF16), pltpu.VMEM((CHUNKS, 16, 128), BF16)),
        in_specs=[hbm] * 10,
        out_specs=(vmem, vmem),
        scratch_shapes=[
            pltpu.SMEM((1, 32), jnp.int32),
            f32(1, LATENT),
            b16(TOK, LATENT),
            b16(64, TOK),
            b16(384, 256),
            pltpu.VMEM((1, 256), jnp.int32),
            pltpu.VMEM((1, 256), jnp.int32),
            b16(STEPS, TOK, QWIDE),
            b16(STEPS, LATENT, WIDE),
            b16(STEPS, LATENT, WIDE),
            b16(2 * TOK, LATENT),
            b16(2 * TOK, TOK),
            b16(TOK, TOK),
            f32(TOK, TOK),
            f32(TOK, TOK),
            f32(TOK, TOK),
            b16(TOK, TOK),
            b16(TOK, TOK),
            f32(TILES, TOK, 128),
            b16(CHUNKS, 8, 128),
            b16(128, 8, 128),
            f32(1024, 128),
            f32(2048, 128),
            b16(128, 16, 128),
            b16(CHUNKS, 16, 128),
            b16(512, 256),
            b16(HEADS_STEP, TOK, 256),
            b16(HEADS_STEP, TOK, 256),
            b16(HEADS_STEP, 256, 256),
            b16(HEADS_STEP, 256, 256),
            b16(HEADS_STEP, 256, 256),
            b16(HEADS_STEP, 256, 256),
            f32(HEADS_STEP, TOK, TOK),
            b16(HEADS_STEP, TOK, 256),
            dma((7,)),
            dma((STEPS,)),
            dma((STEPS,)),
            dma((STEPS,)),
            dma((2,)),
            dma((2,)),
            dma,
            dma,
            dma,
            dma,
        ],
        compiler_params=pltpu.CompilerParams(
            collective_id=0, has_side_effects=True, vmem_limit_bytes=44 * 2**20
        ),
        name="prefill_and_pages",
    )(
        *(
            pltpu.with_memory_space_constraint(x, pltpu.HBM)
            for x in (
                request_lengths,
                kv_gain.reshape(1, LATENT),
                latent_raw,
                rope_raw.T,
                jnp.asarray(trig_table()),
                page_owner.reshape(1, 256),
                page_slot.reshape(1, 256),
                query,
                w_uk,
                w_uv,
            )
        )
    )
    return pl.pallas_call(
        written,
        out_shape=shapes,
        in_specs=[vmem] * 2,
        out_specs=(hbm, hbm),
        scratch_shapes=[f32(CHUNKS * 16, 128), b16(4, PAGE_W), dma((5,))],
        name="results_out",
    )(
        pltpu.with_memory_space_constraint(attended, pltpu.VMEM), pltpu.with_memory_space_constraint(chunks, pltpu.VMEM)
    )


def solution(mesh):
    rows = P(("group", "seq"), None)
    return jax.shard_map(
        on_device,
        mesh=mesh,
        in_specs=(rows, rows, rows, P(), P(), P(), P("group", None), P(), P()),
        out_specs=(rows, rows),
        check_vma=False,
    )
```
